128 devices in a mesh: grp: 2 (over z_hi), dp: 64 (over z_lo, y, x, core).
Axes of the slice: x: 4, y: 4, z: 4 (z_hi: 2, z_lo: 2; z = z_hi * 2 + z_lo), core: 2. Of those that a mesh axis runs over, the one named last changes fastest.
Arguments:
- teacher_hidden: bfloat16 [256, 256, 1024], P(('grp', 'dp')), may hold values from -6 to 6
- passage_len: int32 [256], P(('grp', 'dp')), may hold values from 56 to 224
- qkv_weight: bfloat16 [1024, 3072], P('dp'), may hold values from -0.1875 to 0.1875
- out_weight: bfloat16 [1024, 1024], P(None, 'dp'), may hold values from -0.1875 to 0.1875
- teacher_gain: float32 [1024], replicated, may hold values from 0.25 to 1.75
- score_weight: float32 [1024], replicated, may hold values from -0.375 to 0.375
- query_tokens: bfloat16 [8, 32, 768], replicated, may hold values from -6 to 6
- passage_tokens: bfloat16 [256, 224, 768], P(('grp', 'dp')), may hold values from -6 to 6
- w_in: bfloat16 [768, 3072], replicated, may hold values from -0.21875 to 0.21875
- w_out: bfloat16 [3072, 768], replicated, may hold values from -0.109375 to 0.109375
Outputs:
- teacher_scores: float32 [256], P(('grp', 'dp'))
- grad_in: float32 [768, 3072], P(('grp', 'dp'))
- grad_out: float32 [3072, 768], P(('grp', 'dp'))
The draws below stay inside these ranges and needn't reach their ends.
All inputs are finite; a program needn't handle non-finite values.
Results may differ from the reference program's by a relative error of at most 0.027.
Values may be sent and summed in bfloat16 or wider, within the bound.
No kernel may reach another device: no remote copies, remote signals or barrier semaphores. Data moves between devices by JAX's collectives and lax.ppermute only.
A program may use at most 128 MiB of HBM per device.

```python
import jax
import jax.numpy as jnp
from jax import lax

DT = 1024
HD = 64
DS = 768
FF = 3072
SQ = 32
SP = 224
S = 256
CANDS = 32
P_DEV = 2
PAIRS = 256
QUERIES = 8


def set_ends(array, stream_key, least, high):
    spot = [jax.random.randint(jax.random.fold_in(stream_key, axis), (), 0, length) for axis, length in enumerate(array.shape)]
    widest = array.shape.index(max(array.shape))
    next_to = spot[:widest] + [(spot[widest] + 1) % array.shape[widest]] + spot[widest + 1:]
    return array.at[tuple(spot)].set(least).at[tuple(next_to)].set(high)


def shard_levels(rng, extent, split, low, largest):
    gain = 1.0
    for dim, blocks in split:
        steps = jax.random.uniform(jax.random.fold_in(jax.random.fold_in(rng, 6), dim), (blocks,), jnp.float32, low / len(split), largest / len(split))
        gain = gain * jnp.repeat(jnp.exp(steps), extent[dim] // blocks).reshape((-1,) + (1,) * (len(extent) - 1 - dim))
    return gain


def gaussian(rng, dims, deviation, bound, split=(), dtype=jnp.bfloat16):
    values = deviation * jax.random.normal(rng, dims, jnp.float32)
    if split:
        values = values * shard_levels(rng, dims, split, -0.22, 0.18)
    return jnp.clip(values, -bound, bound).astype(dtype)


def setup_inputs(seed: int = 0) -> dict:
    seeds = jax.random.split(jax.random.key(seed), 11)
    teacher_hidden = gaussian(seeds[0], (PAIRS, S, DT), 1.0, 6.0, ((0, 128),))
    passage_len = set_ends(jax.random.randint(seeds[1], (PAIRS,), SP // 4, SP + 1), jax.random.fold_in(seeds[1], 1), SP // 4, SP).astype(jnp.int32)
    qkv_weight = gaussian(seeds[2], (DT, 3 * DT), DT ** -0.5, 0.1875, ((0, 64),))
    out_weight = gaussian(seeds[3], (DT, DT), DT ** -0.5, 0.1875, ((1, 64),))
    teacher_gain = jnp.clip(1.0 + 0.15 * jax.random.normal(seeds[4], (DT,), jnp.float32), 0.25, 1.75)
    score_weight = gaussian(seeds[5], (DT,), (DT // 4) ** -0.5, 0.375, (), jnp.float32)
    query_tokens = gaussian(seeds[6], (QUERIES, SQ, DS), 1.0, 6.0)
    passage_tokens = gaussian(seeds[7], (PAIRS, SP, DS), 1.0, 6.0, ((0, 128),))
    w_in = gaussian(seeds[8], (DS, FF), DS ** -0.5, 0.21875)
    w_out = gaussian(seeds[9], (FF, DS), FF ** -0.5, 0.109375)
    return {"teacher_hidden": teacher_hidden, "passage_len": passage_len, "qkv_weight": qkv_weight, "out_weight": out_weight, "teacher_gain": teacher_gain, "score_weight": score_weight, "query_tokens": query_tokens, "passage_tokens": passage_tokens, "w_in": w_in, "w_out": w_out}


LOSS_SCALE = 8.0

def normalize(values):
    average = lax.optimization_barrier(jnp.mean(values, -1, keepdims=True))
    centred = values - average
    return centred * lax.rsqrt(lax.optimization_barrier(jnp.mean(centred * centred, -1, keepdims=True)) + 1e-05)

def teacher_pass(teacher_hidden, passage_len, qkv_weight, out_weight, teacher_gain, score_weight):
    pair_count, seq_len, features = teacher_hidden.shape
    head_count = features // HD
    flat_rows = teacher_hidden.reshape(pair_count * seq_len, features)
    key_val = jnp.dot(flat_rows, qkv_weight[:, features:], preferred_element_type=jnp.float32).astype(jnp.bfloat16)
    key_val = key_val.reshape(pair_count, seq_len, 2, head_count, HD)
    leading = teacher_hidden[:, 0, :]
    query_vec = jnp.dot(leading, qkv_weight[:, :features], preferred_element_type=jnp.float32).astype(jnp.bfloat16)
    query_vec = query_vec.reshape(pair_count, head_count, HD)
    logits = jnp.einsum('phd,pshd->phs', query_vec.astype(jnp.float32), key_val[:, :, 0].astype(jnp.float32)) * HD ** (-0.5)
    positions = jnp.arange(seq_len)
    live = (positions[None, :] < SQ) | (positions[None, :] - SQ < passage_len[:, None])
    logits = jnp.where(live[:, None, :], logits, -1e+30)
    attn_weights = jax.nn.softmax(logits, -1).astype(jnp.bfloat16)
    context = jnp.einsum('phs,pshd->phd', attn_weights.astype(jnp.float32), key_val[:, :, 1].astype(jnp.float32))
    context = context.astype(jnp.bfloat16).reshape(pair_count, features)
    projected = jnp.dot(context, out_weight, preferred_element_type=jnp.float32)
    hidden = normalize(leading.astype(jnp.float32) + projected) * teacher_gain
    return lax.optimization_barrier(jnp.sum(hidden * score_weight, -1))

def student_forward(own_query, passages, w_in, w_out):
    tok_rows = jnp.concatenate([own_query.reshape(-1, own_query.shape[2]), passages.reshape(-1, passages.shape[2])], 0)
    preact = jnp.dot(tok_rows, w_in, preferred_element_type=jnp.float32)
    activated = jax.nn.gelu(preact, approximate=False).astype(jnp.bfloat16)
    outputs = tok_rows.astype(jnp.float32) + jnp.dot(activated, w_out, preferred_element_type=jnp.float32)
    return (tok_rows, preact, activated, outputs)

def pooled_scores(outputs, lengths):
    count = lengths.shape[0]
    width = outputs.shape[1]
    query_vec = normalize(lax.optimization_barrier(jnp.mean(outputs[:count * SQ].reshape(count, SQ, width), 1)))
    passage_part = outputs[count * SQ:].reshape(count, -1, width)
    positions = jnp.arange(passage_part.shape[1])
    weights = (positions[None, :] < lengths[:, None]).astype(jnp.float32) / lengths[:, None].astype(jnp.float32)
    passage_vec = normalize(lax.optimization_barrier(jnp.sum(passage_part * weights[:, :, None], 1)))
    return lax.optimization_barrier(jnp.sum(passage_vec * query_vec, -1)) * width ** (-0.5)

def student_backward(preact, outputs, lengths, cotangent, w_out):
    _, pull_scores = jax.vjp(lambda states: pooled_scores(states, lengths), outputs)
    grad_tokens = pull_scores(cotangent)[0].astype(jnp.bfloat16)
    grad_act = lax.dot_general(grad_tokens, w_out, (((1,), (1,)), ((), ())), preferred_element_type=jnp.float32)
    _, pull_gelu = jax.vjp(lambda values: jax.nn.gelu(values, approximate=False), preact)
    grad_pre = pull_gelu(grad_act)[0].astype(jnp.bfloat16)
    return (grad_tokens, grad_pre)

def reference(teacher_hidden, passage_len, qkv_weight, out_weight, teacher_gain, score_weight, query_tokens, passage_tokens, w_in, w_out):
    teacher = teacher_pass(teacher_hidden, passage_len, qkv_weight, out_weight, teacher_gain, score_weight)
    blocks = PAIRS // P_DEV
    per_block = passage_tokens.reshape(blocks, P_DEV, SP, DS)
    lengths = passage_len.reshape(blocks, P_DEV)
    owners = (jnp.arange(PAIRS) % QUERIES).astype(jnp.int32).reshape(blocks, P_DEV)

    def forward_step(unused, inputs):
        owner_ids, passages, block_len = inputs
        outputs = student_forward(query_tokens[owner_ids], passages, w_in, w_out)[3]
        return (unused, pooled_scores(outputs, block_len))
    _, student = lax.scan(forward_step, jnp.zeros((), jnp.float32), (owners, per_block, lengths))
    student = student.reshape(PAIRS)
    lse_t = jax.nn.logsumexp(teacher.reshape(CANDS, QUERIES), 0)
    lse_s = jax.nn.logsumexp(student.reshape(CANDS, QUERIES), 0)
    pair_query = jnp.arange(PAIRS) % QUERIES
    cotangent = LOSS_SCALE * (jnp.exp(student - lse_s[pair_query]) - jnp.exp(teacher - lse_t[pair_query]))

    def backward_step(sums, inputs):
        owner_ids, passages, block_len, block_cot = inputs
        tok_rows, preact, activated, outputs = student_forward(query_tokens[owner_ids], passages, w_in, w_out)
        grad_tokens, grad_pre = student_backward(preact, outputs, block_len, block_cot, w_out)
        term_in = lax.dot_general(tok_rows, grad_pre, (((0,), (0,)), ((), ())), preferred_element_type=jnp.float32)
        term_out = lax.dot_general(activated, grad_tokens, (((0,), (0,)), ((), ())), preferred_element_type=jnp.float32)
        return ((sums[0] + term_in, sums[1] + term_out), None)
    zero_sums = (jnp.zeros((DS, FF), jnp.float32), jnp.zeros((FF, DS), jnp.float32))
    (grad_in, grad_out), _ = lax.scan(backward_step, zero_sums, (owners, per_block, lengths, cotangent.reshape(blocks, P_DEV)))
    return (teacher, grad_in, grad_out)
```

```python
import jax
import jax.numpy as jnp
from jax import lax
from jax.experimental import pallas as pl
from jax.experimental.pallas import tpu as pltpu
from jax.sharding import Mesh
from jax.sharding import PartitionSpec as P

HD = 64
SQ = 32
SP = 224
S = SQ + SP
DT = 1024
DS = 768
FF = 3072
CHIPS = 64
QUARTER = 4 * HD
WIDE = 3 * DS
PAY = WIDE + 128 + DS // 2
EPS = 1e-05
LOSS_SCALE = 8.0
MIB = 1 << 20

AXES = ("zh", "zl", "y", "xh", "xl", "c")
DP = ("zl", "y", "xh", "xl", "c")
X = ("xh", "xl")
CHIP_AXES = ("zh", "zl", "y", "xh", "xl")
RIVALS = ("zh", "zl", "y", "xh")
SWAP = [(0, 1), (1, 0)]
BOTH = [(0, 3), (1, 2), (2, 1), (3, 0)]

F32 = jnp.float32
BF16 = jnp.bfloat16
NT = (((1,), (1,)), ((), ()))


def params(mib):
    return pltpu.CompilerParams(vmem_limit_bytes=mib * MIB)


def ring(step):
    return [(i, (i + step) % 4) for i in range(4)]


def mm(a, b):
    return jnp.dot(a, b, preferred_element_type=F32)


def mm_nt(a, b):
    return lax.dot_general(a, b, NT, preferred_element_type=F32)


def iota(shape, dim):
    return lax.broadcasted_iota(jnp.int32, shape, dim)


def send_axis(piece, axis):
    return [piece] + [lax.ppermute(piece, axis, ring(step)) for step in (1, 3, 2)]


def join_axis(pieces, axis, dim):
    here, piece = lax.axis_index(axis), pieces[0]
    shape = piece.shape[:dim] + (4,) + piece.shape[dim + 1 :]
    whole = jnp.zeros(shape, piece.dtype)
    for part, step in zip(pieces, (0, 1, 3, 2)):
        start = [0] * len(shape)
        start[dim] = (here - step) % 4
        whole = lax.dynamic_update_slice(whole, part, tuple(start))
    return whole


def forward_kernel(
    lens, q_ref, p_ref, win_hbm, wout_hbm, sums_tiles, g_ref, gp_hbm,
    rows, win, wout, slope, pulled_ref, sums_ref, gp, in_sems, out_sems, wout_sem,
):
    def load(j):
        cols = pl.ds(pl.multiple_of(j * 512, 512), 512)
        return pltpu.make_async_copy(win_hbm.at[:, cols], win.at[:, cols], in_sems.at[j])

    def save(j):
        cols = pl.ds(pl.multiple_of(j * DS, DS), DS)
        return pltpu.make_async_copy(gp.at[:, :, cols], gp_hbm.at[:, :, cols], out_sems.at[j])

    load_out = pltpu.make_async_copy(wout_hbm, wout, wout_sem)
    for j in range(6):
        load(j).start()
    load_out.start()
    for i in range(2):
        rows[i * S : i * S + SQ] = q_ref[i]
        rows[i * S + SQ : (i + 1) * S] = p_ref[i]
    group, slot = iota((8, 2 * S), 0), iota((8, 2 * S), 1)
    at = slot % S
    length = jnp.where(slot < S, lens[0], lens[1])
    live = at - SQ < length
    side = jnp.where(at < SQ, 0, 1)
    pool = jnp.where((group == 2 * (slot // S) + side) & live, 1.0, 0.0).astype(BF16)

    def forward(j, carry):
        load(j).wait()
        for part in range(2):
            cols = pl.ds(pl.multiple_of(j * 512 + part * 256, 256), 256)
            pre = mm(rows[...], win[:, cols])
            bell = jnp.exp(pre * pre * -0.5)
            denominator = 1.0 + jnp.abs(pre) * (0.3275911 * 0.7071067811865476)
            t = pl.reciprocal(denominator, approx=True)
            t = t * (2.0 - denominator * t)
            poly = 0.5 * 1.061405429 * t - 0.5 * 1.453152027
            poly = poly * t + 0.5 * 1.421413741
            poly = poly * t - 0.5 * 0.284496736
            poly = poly * t + 0.5 * 0.254829592
            tail = poly * t * bell
            cdf = jnp.where(pre < 0.0, tail, 1.0 - tail)
            act = (pre * cdf).astype(BF16)
            slope[:, cols] = cdf + pre * bell * 0.3989422804014327
            sums_ref[:, cols] = mm(pool, act)
        return carry

    lax.fori_loop(0, FF // 512, forward, 0)
    load_out.wait()
    sums = sums_ref[...]
    high = sums.astype(BF16)
    low = (sums - high.astype(F32)).astype(BF16)
    out = mm(jnp.concatenate([high, low], 0), wout[...])
    row8 = iota((8, 1), 0)
    count = jnp.where(row8 % 2 == 0, SQ, jnp.where(row8 < 2, lens[0], lens[1])).astype(F32)
    means = (mm(pool, rows[...]) + out[:8] + out[8:]) / count
    means = means[:4]
    centred = means - jnp.mean(means, -1, keepdims=True)
    scale = lax.rsqrt(jnp.mean(centred * centred, -1, keepdims=True) + EPS)
    unit = centred * scale
    other = jnp.concatenate([unit[1:2], unit[0:1], unit[3:4], unit[2:3]], 0)
    cross = jnp.sum(unit * other, -1, keepdims=True) * DS ** (-0.5)
    back = other * DS ** (-0.5)
    back = scale * (
        back
        - jnp.mean(back, -1, keepdims=True)
        - unit * jnp.mean(back * unit, -1, keepdims=True)
    )
    grad = (back / count[:4]).astype(BF16)
    g_ref[...] = grad
    grad8 = jnp.concatenate([grad, jnp.zeros((4, DS), BF16)], 0)
    pulled_ref[...] = mm_nt(grad8, wout[...])
    at_row = iota((S, 1), 0) - SQ

    def backward(j, carry):
        for part in range(3):
            cols = pl.ds(pl.multiple_of(j * DS + part * 256, 256), 256)
            pulled = pulled_ref[:, cols]
            for i in range(2):
                gate = jnp.where(at_row < lens[i], pulled[2 * i + 1 : 2 * i + 2], 0.0)
                gp[i, SQ:, cols] = (gate[SQ:] * slope[i * S + SQ : (i + 1) * S, cols]).astype(BF16)
                gp[i, :SQ, cols] = (
                    pulled[2 * i : 2 * i + 1] * slope[i * S : i * S + SQ, cols]
                ).astype(BF16)
        save(j).start()
        return carry

    lax.fori_loop(0, FF // DS, backward, 0)
    score = jnp.broadcast_to(cross, (4, 16))
    for d in range(CHIPS):
        part = sums[:4, d * 48 : d * 48 + 48]
        sums_tiles[d] = jnp.concatenate([part, score, part, score], 1)
    for j in range(FF // DS):
        save(j).wait()


def student_forward(lens, own_query, passages, w_in, w_out):
    vmem = pl.BlockSpec(memory_space=pltpu.VMEM)
    anywhere = pl.BlockSpec(memory_space=pl.ANY)
    return pl.pallas_call(
        forward_kernel,
        out_shape=(
            jax.ShapeDtypeStruct((CHIPS, 4, 128), F32),
            jax.ShapeDtypeStruct((4, DS), BF16),
            jax.ShapeDtypeStruct((2, S, FF), BF16),
        ),
        in_specs=[pl.BlockSpec(memory_space=pltpu.SMEM), vmem, vmem, anywhere, anywhere],
        out_specs=(vmem, vmem, anywhere),
        scratch_shapes=[
            pltpu.VMEM((2 * S, DS), BF16),
            pltpu.VMEM((DS, FF), BF16),
            pltpu.VMEM((FF, DS), BF16),
            pltpu.VMEM((2 * S, FF), F32),
            pltpu.VMEM((8, FF), F32),
            pltpu.VMEM((8, FF), F32),
            pltpu.VMEM((2, S, FF), BF16),
            pltpu.SemaphoreType.DMA((6,)),
            pltpu.SemaphoreType.DMA((4,)),
            pltpu.SemaphoreType.DMA,
        ],
        compiler_params=params(56),
        cost_estimate=pl.CostEstimate(flops=1, bytes_accessed=1, transcendentals=0),
        name="student_forward",
    )(lens, own_query, passages, w_in, w_out)


def weight_grad_kernel(half_ref, q_ref, p_ref, gp_ref, out_ref):
    half = half_ref[0]

    def select(first):
        line, feature = iota((8 * CHIPS, DS), 0), iota((8 * CHIPS, DS), 1)
        lane = line % 8
        if first is None:
            wanted = jnp.where(lane < 6, (2 * (line // 8) + half) * 6 + lane, -1)
        else:
            wanted = jnp.where(lane < 6, -1, (2 * (line // 8) + half) * 6 + first + 3 * (lane - 6))
        return jnp.where(feature == wanted, 1.0, 0.0).astype(BF16)

    rows = [jnp.concatenate([q_ref[i], p_ref[i]], 0) for i in range(2)]
    main = select(None)
    main = [mm_nt(main, rows[i]).astype(BF16) for i in range(2)]
    for k in range(3):
        tail = select(k)
        for i in range(2):
            rest = mm_nt(tail, rows[i]).astype(BF16)
            for part in range(3):
                at = k * DS + part * 256
                late = 3 * DS + part * 256
                out_ref[i, :, at : at + 256] = (
                    mm(main[i], gp_ref[i, :, at : at + 256])
                    + mm(rest, gp_ref[i, :, late : late + 256])
                ).astype(BF16)


def weight_grad(half, own_query, passages, grad_pre, name, flops):
    vmem = pl.BlockSpec(memory_space=pltpu.VMEM)
    return pl.pallas_call(
        weight_grad_kernel,
        out_shape=jax.ShapeDtypeStruct((2, 8 * CHIPS, WIDE), BF16),
        in_specs=[pl.BlockSpec(memory_space=pltpu.SMEM)] + [vmem] * 3,
        out_specs=vmem,
        compiler_params=params(32),
        cost_estimate=pl.CostEstimate(flops=flops, bytes_accessed=flops // 1000, transcendentals=0),
        name=name,
    )(half.reshape(1), own_query, passages, grad_pre)


def turn(values, shift):
    wide = values.shape[1] // 2
    amount = shift * 128
    return jnp.concatenate(
        [pltpu.roll(values[:, :wide], amount, 1), pltpu.roll(values[:, wide:], amount, 1)], 1
    )


def teacher_kernel(
    y_ref, x0, x1, x2, x3, w0, w1, w2, w3, sums_ref, near_ref, flip_ref, far_ref, farflip_ref
):
    xs, ws = (x0, x1, x2, x3), (w0, w1, w2, w3)
    there, back = (4 - y_ref[0]) % 4, y_ref[0]
    blocks = [(ws[m], z, (z * 4 + m) * 128) for z in range(2) for m in range(4)]

    def reduce(values, first):
        total = None
        for ref, z, at in blocks:
            term = mm(values[:, at : at + 128], ref[z, :, first : first + QUARTER])
            total = term if total is None else total + term
        return total

    def expand(values, first):
        return jnp.concatenate(
            [mm_nt(values, ref[z, :, first : first + QUARTER]) for ref, z, _ in blocks], 1
        )

    lead = jnp.concatenate([x[i * S : i * S + 1] for x in xs for i in range(2)], 0).astype(F32)
    query = reduce(turn(lead, there).astype(BF16), 0).astype(BF16).astype(F32)
    head, col = iota((32, QUARTER), 0) // 8, iota((32, QUARTER), 1) // HD
    spread = jnp.where(head == col, jnp.concatenate([query] * 4, 0), 0.0).astype(BF16)
    keyed = turn(expand(spread, QUARTER), back).astype(BF16)
    logits = jnp.concatenate([mm_nt(keyed, x[: 2 * S]) for x in xs], 1) * HD ** (-0.5)
    live = jnp.concatenate([x[2 * S : 2 * S + 1, : 2 * S].astype(F32) for x in xs], 1)
    pair, slot = iota((32, 8 * S), 0) % 8, iota((32, 8 * S), 1) // S
    logits = jnp.where((pair == slot) & (live > 0.5), logits, -1e30)
    weights = jnp.exp(logits - jnp.max(logits, -1, keepdims=True))
    weights = (weights / jnp.sum(weights, -1, keepdims=True)).astype(BF16)
    mixed = mm(weights[:, : 2 * S], x0[: 2 * S])
    for i in range(1, 4):
        mixed += mm(weights[:, i * 2 * S : (i + 1) * 2 * S], xs[i][: 2 * S])
    context = reduce(turn(mixed, there).astype(BF16), 2 * QUARTER)
    context = jnp.where(head == col, context, 0.0)
    context = (context[:8] + context[8:16] + context[16:24] + context[24:]).astype(BF16)
    projected = turn(expand(context, 3 * QUARTER), back)
    own = projected[:2] + lead[:2]
    near_ref[...] = jnp.concatenate([own, projected[2:4]], 0)
    student = jnp.broadcast_to(sums_ref[0, :, 48:49], (4, DT))
    flip_ref[...] = jnp.concatenate([projected[2:4], own, student], 0)
    far_ref[...] = projected[4:]
    farflip_ref[...] = jnp.concatenate([projected[6:], projected[4:6]], 0)


def teacher_partial(y, xs, ws, sums):
    shape = jax.ShapeDtypeStruct((4, DT), F32)
    vmem = pl.BlockSpec(memory_space=pltpu.VMEM)
    return pl.pallas_call(
        teacher_kernel,
        out_shape=(shape, jax.ShapeDtypeStruct((8, DT), F32), shape, shape),
        in_specs=[pl.BlockSpec(memory_space=pltpu.SMEM)] + [vmem] * 9,
        out_specs=(vmem,) * 4,
        compiler_params=params(32),
        cost_estimate=pl.CostEstimate(flops=10**9, bytes_accessed=6 * 10**6, transcendentals=0),
        name="teacher_partial",
    )(y.reshape(1), *xs, *ws, sums)


def score_kernel(a, b, c, d, gain, weight, sums_ref, tile_ref, spread_ref):
    values = a[...] + b[:4] + c[...] + d[...]
    centred = values - jnp.mean(values, -1, keepdims=True)
    unit = centred * lax.rsqrt(jnp.mean(centred * centred, -1, keepdims=True) + EPS)
    score = jnp.sum(unit * gain[...] * weight[...], -1, keepdims=True)
    own, got = sums_ref[0, :, 48:49], b[4:, :1]
    student = jnp.concatenate([own[0:1], own[2:3], got[0:1], got[2:3]], 0)
    student = jnp.broadcast_to(student, (4, 128))
    tile = jnp.concatenate([jnp.broadcast_to(score, (4, 128)), student], 0)
    tile_ref[...] = tile
    for i in range(32):
        spread_ref[i] = tile


def score_tile(parts, gain, weight, sums):
    vmem = pl.BlockSpec(memory_space=pltpu.VMEM)
    return pl.pallas_call(
        score_kernel,
        out_shape=(
            jax.ShapeDtypeStruct((8, 128), F32),
            jax.ShapeDtypeStruct((32, 8, 128), F32),
        ),
        in_specs=[vmem] * 7,
        out_specs=(vmem,) * 2,
        name="score_tile",
    )(*parts, gain, weight, sums)


def payload_kernel(tile_ref, all_ref, mine_ref, recv_ref, sums_ref, g_ref, out_ref, cot_ref):
    @pl.when(pl.program_id(0) == 0)
    def _():
        every = all_ref[...]
        top = jnp.max(every, 0)
        lse = top + jnp.log(jnp.sum(jnp.exp(every - top[None]), 0))
        share = jnp.exp(tile_ref[...] - lse)
        cot = LOSS_SCALE * (share[4:] - share[:4])
        cot_ref[...] = jnp.concatenate([cot[j : j + 1] for j in range(4) for _ in range(2)], 0)

    cot = cot_ref[...]
    total = None
    for ref, base in ((mine_ref, 0), (recv_ref, 4)):
        for i in range(2):
            term = ref[i].astype(F32) * cot[base + 2 * i : base + 2 * i + 1, :1]
            total = term if total is None else total + term
    out_ref[:, :, :WIDE] = total.reshape(8, 8, WIDE).astype(BF16)
    scaled = sums_ref[...] * cot[None, :4]
    high = scaled.astype(BF16).astype(F32)
    scaled = jnp.where(iota((8, 4, 128), 2) < 64, high, scaled - high)
    out_ref[:, :, WIDE : WIDE + 128] = jnp.concatenate([scaled, scaled], 1).astype(BF16)
    grad = g_ref[...].astype(F32)
    grad = jnp.concatenate([grad[:, : DS // 2], grad[:, DS // 2 :]], 0).astype(BF16)
    out_ref[:, :, WIDE + 128 :] = jnp.broadcast_to(grad[None], (8, 8, DS // 2))


def payload(tile, every, mine, received, sums, grad):
    whole = lambda *shape: pl.BlockSpec(shape, lambda i: (0,) * len(shape))
    half = pl.BlockSpec((2, 64, WIDE), lambda i: (0, i, 0))
    return pl.pallas_call(
        payload_kernel,
        grid=(8,),
        out_shape=jax.ShapeDtypeStruct((CHIPS, 8, PAY), BF16),
        in_specs=[
            whole(8, 128),
            whole(32, 8, 128),
            half,
            half,
            pl.BlockSpec((8, 4, 128), lambda i: (i, 0, 0)),
            whole(4, DS),
        ],
        out_specs=pl.BlockSpec((8, 8, PAY), lambda i: (i, 0, 0)),
        scratch_shapes=[pltpu.VMEM((8, 128), F32)],
        compiler_params=params(56),
        name="payload",
    )(tile, every, mine, received, sums, grad)


def final_kernel(core_ref, in_ref, gin_ref, own_ref, send_ref):
    total = in_ref[0, :, :WIDE].astype(F32)
    for d in range(1, CHIPS):
        total += in_ref[d, :, :WIDE].astype(F32)
    gin_ref[:, :WIDE] = total[:6]
    for r in range(6):
        line, at = 6 + r // 3, r % 3 * DS
        gin_ref[r : r + 1, WIDE:] = total[line : line + 1, at : at + DS]
    columns = in_ref[:, :, WIDE : WIDE + 128].astype(F32).reshape(CHIPS * 8, 128).T
    line = iota((128, CHIPS * 8), 1) % 8
    grads = in_ref[:, :, WIDE + 128 :].astype(F32).reshape(CHIPS * 8, DS // 2).astype(BF16)
    left = mm(jnp.where(line < 4, columns, 0.0).astype(BF16), grads)
    right = mm(jnp.where(line < 4, 0.0, columns).astype(BF16), grads)
    both = jnp.concatenate([left[:48] + left[64:112], right[:48] + right[64:112]], 1)
    first = core_ref[0] == 0
    own_ref[...] = jnp.where(first, both[:24], both[24:])
    send_ref[...] = jnp.where(first, both[24:], both[:24])


def final(core, incoming):
    vmem = pl.BlockSpec(memory_space=pltpu.VMEM)
    part = jax.ShapeDtypeStruct((24, DS), F32)
    return pl.pallas_call(
        final_kernel,
        out_shape=(jax.ShapeDtypeStruct((6, FF), F32), part, part),
        in_specs=[pl.BlockSpec(memory_space=pltpu.SMEM), vmem],
        out_specs=(vmem,) * 3,
        compiler_params=params(32),
        name="final",
    )(core.reshape(1), incoming)


def exchange_weights(qkv_weight, out_weight):
    zl, core = lax.axis_index("zl"), lax.axis_index("c")
    me = 2 * zl + core
    heads = qkv_weight.reshape(16, 3, 4, QUARTER).transpose(2, 0, 1, 3).reshape(4, 16, 3 * QUARTER)
    outs = out_weight.T.reshape(16, 4, QUARTER).transpose(1, 0, 2)
    packed = jnp.concatenate([heads, outs], -1)
    pick = lambda index: lax.dynamic_index_in_dim(packed, index, 0, keepdims=True)
    mine = pick(me)
    from_core = lax.ppermute(pick(me ^ 1), "c", SWAP)
    from_far = lax.ppermute(pick(me ^ 2), "zl", SWAP)
    from_both = lax.ppermute(pick(me ^ 3), ("zl", "c"), BOTH)
    four = jnp.zeros((4, 16, DT), BF16)
    for part, who in ((mine, me), (from_core, me ^ 1), (from_far, me ^ 2), (from_both, me ^ 3)):
        four = lax.dynamic_update_slice(four, part, (who, 0, 0))
    return four.reshape(2, 1, 1, 32, DT)


def body(
    teacher_hidden,
    passage_len,
    qkv_weight,
    out_weight,
    teacher_gain,
    score_weight,
    query_tokens,
    passage_tokens,
    w_in,
    w_out,
):
    core = lax.axis_index("c")
    first = lax.axis_index("xl") * 4 + core * 2

    slots = jnp.arange(S)
    live = (slots[None, :] < SQ) | (slots[None, :] - SQ < passage_len[:, None])
    live = jnp.pad(live.astype(BF16).reshape(1, 2 * S), ((0, 15), (0, DT - 2 * S)))
    hidden = jnp.concatenate([teacher_hidden.reshape(2 * S, DT), live], 0)
    own_query = lax.dynamic_slice_in_dim(query_tokens, first, 2, 0)

    four = exchange_weights(qkv_weight, out_weight)
    four, hidden = lax.optimization_barrier((four, hidden))
    hidden_far = lax.ppermute(hidden, "zl", SWAP)
    hidden_core = lax.ppermute(hidden, "c", SWAP)
    plane = join_axis(send_axis(four, X), X, 2)
    plane, own_query, hidden_core = lax.optimization_barrier((plane, own_query, hidden_core))
    planes = send_axis(plane, "y")

    sums, grad, grad_pre = student_forward(passage_len, own_query, passage_tokens, w_in, w_out)
    other = weight_grad(1 - core, own_query, passage_tokens, grad_pre, "weight_grad_other", 1)

    planes, other, hidden_far = lax.optimization_barrier((planes, other, hidden_far))
    hidden_both = lax.ppermute(hidden_far, "c", SWAP)
    here, before, after, across = [part.reshape(2, 128, DT) for part in planes]
    near, flip, far, farflip = teacher_partial(
        lax.axis_index("y"),
        (hidden, hidden_core, hidden_far, hidden_both),
        (here, after, across, before),
        sums,
    )
    parts = (
        near,
        lax.ppermute(flip, "c", SWAP),
        lax.ppermute(far, "zl", SWAP),
        lax.ppermute(farflip, ("zl", "c"), BOTH),
    )
    other, _ = lax.optimization_barrier((other, near))
    received = lax.ppermute(other, "c", SWAP)
    tile, spread = score_tile(parts, teacher_gain[None], score_weight[None], sums)
    every = lax.all_to_all(spread, RIVALS, 0, 0, tiled=True)
    late_query, _ = lax.optimization_barrier((own_query, tile))
    mine = weight_grad(core, late_query, passage_tokens, grad_pre, "weight_grad_mine", 6 * 10**9)
    outgoing = payload(tile, every, mine, received, sums, grad)
    outgoing, teacher = lax.optimization_barrier((outgoing, tile[:2, 0]))
    incoming = lax.all_to_all(outgoing, CHIP_AXES, 0, 0, tiled=True)
    grad_in, own_out, send_out = final(core, incoming)
    return (teacher, grad_in, own_out + lax.ppermute(send_out, "c", SWAP))


def solution(mesh):
    fine = Mesh(mesh.devices.reshape(2, 2, 4, 2, 2, 2), AXES)
    placed = (
        P(AXES, None, None),
        P(AXES),
        P(DP, None),
        P(None, DP),
        P(),
        P(),
        P(),
        P(AXES, None, None),
        P(),
        P(),
    )
    return jax.shard_map(
        body,
        mesh=fine,
        in_specs=placed,
        out_specs=(P(AXES), P(AXES, None), P(AXES, None)),
        check_vma=False,
    )
```

```python
import jax
import jax.numpy as jnp
from jax import lax
from jax.experimental import pallas as pl
from jax.experimental.pallas import tpu as pltpu
from jax.sharding import Mesh
from jax.sharding import PartitionSpec as P

HD = 64
SQ = 32
SP = 224
S = SQ + SP
DT = 1024
DS = 768
FF = 3072
CHIPS = 64
QUARTER = 4 * HD
WIDE = 3 * DS
PAY = WIDE + 128 + DS // 2
EPS = 1e-05
LOSS_SCALE = 8.0
MIB = 1 << 20

AXES = ("zh", "zl", "y", "xh", "xl", "c")
DP = ("zl", "y", "xh", "xl", "c")
X = ("xh", "xl")
CHIP_AXES = ("zh", "zl", "y", "xh", "xl")
RIVALS = ("zh", "y", "xh")
SWAP = [(0, 1), (1, 0)]
BOTH = [(0, 3), (1, 2), (2, 1), (3, 0)]

F32 = jnp.float32
BF16 = jnp.bfloat16
NT = (((1,), (1,)), ((), ()))


def params(mib):
    return pltpu.CompilerParams(vmem_limit_bytes=mib * MIB)


def ring(step):
    return [(i, (i + step) % 4) for i in range(4)]


def mm(a, b):
    return jnp.dot(a, b, preferred_element_type=F32)


def mm_nt(a, b):
    return lax.dot_general(a, b, NT, preferred_element_type=F32)


def iota(shape, dim):
    return lax.broadcasted_iota(jnp.int32, shape, dim)


def send_axis(piece, axis):
    return [piece] + [lax.ppermute(piece, axis, ring(step)) for step in (1, 3, 2)]


def join_axis(pieces, axis, dim):
    here, piece = lax.axis_index(axis), pieces[0]
    shape = piece.shape[:dim] + (4,) + piece.shape[dim + 1 :]
    whole = jnp.zeros(shape, piece.dtype)
    for part, step in zip(pieces, (0, 1, 3, 2)):
        start = [0] * len(shape)
        start[dim] = (here - step) % 4
        whole = lax.dynamic_update_slice(whole, part, tuple(start))
    return whole


def student_kernel(
    lens, q_ref, p_ref, win_hbm, wout_hbm, sums_tiles, g_ref, gp_hbm, other_hbm,
    rows, win, wout, slope, pulled_ref, sums_ref, gp, blocks, in_sems, out_sems, wout_sem, other_sems,
):
    def load(j):
        cols = pl.ds(pl.multiple_of(j * 512, 512), 512)
        return pltpu.make_async_copy(win_hbm.at[:, cols], win.at[:, cols], in_sems.at[j])

    def save(j):
        cols = pl.ds(pl.multiple_of(j * DS, DS), DS)
        return pltpu.make_async_copy(gp.at[:, :, cols], gp_hbm.at[:, :, cols], out_sems.at[j])

    def send(i, k):
        cols = pl.ds(k * DS, DS)
        return pltpu.make_async_copy(
            blocks.at[i, :, cols], other_hbm.at[i, :, cols], other_sems.at[i * 3 + k]
        )

    load_out = pltpu.make_async_copy(wout_hbm, wout, wout_sem)
    for j in range(6):
        load(j).start()
    load_out.start()
    for i in range(2):
        rows[i * S : i * S + SQ] = q_ref[i]
        rows[i * S + SQ : (i + 1) * S] = p_ref[i]
    at_row = iota((S, 1), 0) - SQ

    def pool(values):
        sums = []
        for i in range(2):
            part = values[i * S : (i + 1) * S].astype(F32)
            sums.append(jnp.sum(part[:SQ], 0, keepdims=True))
            part = jnp.where(at_row[SQ:] < lens[i], part[SQ:], 0.0)
            sums.append(jnp.sum(part, 0, keepdims=True))
        return jnp.concatenate(sums + sums, 0)


    def forward(j, carry):
        load(j).wait()
        for part in range(2):
            cols = pl.ds(pl.multiple_of(j * 512 + part * 256, 256), 256)
            pre = mm(rows[...], win[:, cols])
            bell = jnp.exp(pre * pre * -0.5)
            denominator = 1.0 + jnp.abs(pre) * (0.3275911 * 0.7071067811865476)
            t = pl.reciprocal(denominator, approx=True)
            t = t * (2.0 - denominator * t)
            poly = 0.5 * 1.061405429 * t - 0.5 * 1.453152027
            poly = poly * t + 0.5 * 1.421413741
            poly = poly * t - 0.5 * 0.284496736
            poly = poly * t + 0.5 * 0.254829592
            tail = poly * t * bell
            cdf = jnp.where(pre < 0.0, tail, 1.0 - tail)
            act = (pre * cdf).astype(BF16)
            slope[:, cols] = cdf + pre * bell * 0.3989422804014327
            sums_ref[:, cols] = pool(act)
        return carry

    lax.fori_loop(0, FF // 512, forward, 0)
    load_out.wait()
    sums = sums_ref[...]
    high = sums.astype(BF16)
    low = (sums - high.astype(F32)).astype(BF16)
    out = mm(jnp.concatenate([high, low], 0), wout[...])
    row8 = iota((8, 1), 0)
    count = jnp.where(row8 % 2 == 0, SQ, jnp.where(row8 < 2, lens[0], lens[1])).astype(F32)
    means = (pool(rows[...]) + out[:8] + out[8:]) / count
    means = means[:4]
    centred = means - jnp.mean(means, -1, keepdims=True)
    scale = lax.rsqrt(jnp.mean(centred * centred, -1, keepdims=True) + EPS)
    unit = centred * scale
    other = jnp.concatenate([unit[1:2], unit[0:1], unit[3:4], unit[2:3]], 0)
    cross = jnp.sum(unit * other, -1, keepdims=True) * DS ** (-0.5)
    back = other * DS ** (-0.5)
    back = scale * (
        back
        - jnp.mean(back, -1, keepdims=True)
        - unit * jnp.mean(back * unit, -1, keepdims=True)
    )
    grad = (back / count[:4]).astype(BF16)
    g_ref[...] = grad
    grad8 = jnp.concatenate([grad, jnp.zeros((4, DS), BF16)], 0)
    pulled_ref[...] = mm_nt(grad8, wout[...])
    def backward(j, carry):
        for part in range(3):
            cols = pl.ds(pl.multiple_of(j * DS + part * 256, 256), 256)
            pulled = pulled_ref[:, cols]
            for i in range(2):
                gate = jnp.where(at_row < lens[i], pulled[2 * i + 1 : 2 * i + 2], 0.0)
                gp[i, SQ:, cols] = (gate[SQ:] * slope[i * S + SQ : (i + 1) * S, cols]).astype(BF16)
                gp[i, :SQ, cols] = (
                    pulled[2 * i : 2 * i + 1] * slope[i * S : i * S + SQ, cols]
                ).astype(BF16)
        save(j).start()
        return carry

    lax.fori_loop(0, FF // DS, backward, 0)
    score = jnp.broadcast_to(cross, (4, 16))
    for d in range(CHIPS):
        part = sums[:4, d * 48 : d * 48 + 48]
        sums_tiles[d] = jnp.concatenate([part, score, part, score], 1)
    grad_blocks(
        lens[2], rows, gp, blocks, lambda i, k: send(i, k).start()
    )
    for j in range(FF // DS):
        save(j).wait()
    for j in range(6):
        send(j // 3, j % 3).wait()


def student(lens, own_query, passages, w_in, w_out):
    vmem = pl.BlockSpec(memory_space=pltpu.VMEM)
    anywhere = pl.BlockSpec(memory_space=pl.ANY)
    return pl.pallas_call(
        student_kernel,
        out_shape=(
            jax.ShapeDtypeStruct((CHIPS, 4, 128), F32),
            jax.ShapeDtypeStruct((4, DS), BF16),
            jax.ShapeDtypeStruct((2, S, FF), BF16),
            jax.ShapeDtypeStruct((2, 8 * CHIPS, WIDE), BF16),
        ),
        in_specs=[pl.BlockSpec(memory_space=pltpu.SMEM), vmem, vmem, anywhere, anywhere],
        out_specs=(vmem, vmem, anywhere, anywhere),
        scratch_shapes=[
            pltpu.VMEM((2 * S, DS), BF16),
            pltpu.VMEM((DS, FF), BF16),
            pltpu.VMEM((FF, DS), BF16),
            pltpu.VMEM((2 * S, FF), F32),
            pltpu.VMEM((8, FF), F32),
            pltpu.VMEM((8, FF), F32),
            pltpu.VMEM((2, S, FF), BF16),
            pltpu.VMEM((2, 8 * CHIPS, WIDE), BF16),
            pltpu.SemaphoreType.DMA((6,)),
            pltpu.SemaphoreType.DMA((4,)),
            pltpu.SemaphoreType.DMA,
            pltpu.SemaphoreType.DMA((6,)),
        ],
        compiler_params=params(60),
        cost_estimate=pl.CostEstimate(flops=1, bytes_accessed=1, transcendentals=0),
        name="student",
    )(lens, own_query, passages, w_in, w_out)


def select_features(half, rows):
    line, feature = iota((8 * CHIPS, DS), 0), iota((8 * CHIPS, DS), 1)
    lane = line % 8
    wanted = jnp.where(lane < 6, (2 * (line // 8) + half) * 6 + lane, -1)
    return mm_nt(jnp.where(feature == wanted, 1.0, 0.0).astype(BF16), rows)


def late_features(wide, k):
    lane = iota((8 * CHIPS, S), 0) % 8
    return jnp.where(
        lane == 6,
        pltpu.roll(wide, 6 - k, 0),
        jnp.where(lane == 7, pltpu.roll(wide, 4 - k, 0), 0.0),
    ).astype(BF16)


def grad_blocks(half, rows, grad, out, done):
    for i in range(2):
        wide = select_features(half, rows[i * S : (i + 1) * S])
        main = wide.astype(BF16)
        for k in range(3):
            rest = late_features(wide, k)
            for part in range(3):
                at = k * DS + part * 256
                late = 3 * DS + part * 256
                out[i, :, at : at + 256] = (
                    mm(main, grad[i, :, at : at + 256]) + mm(rest, grad[i, :, late : late + 256])
                ).astype(BF16)
            done(i, k)


def turn(values, shift):
    wide = values.shape[1] // 2
    amount = shift * 128
    return jnp.concatenate(
        [pltpu.roll(values[:, :wide], amount, 1), pltpu.roll(values[:, wide:], amount, 1)], 1
    )


def teacher_kernel(
    y_ref, x0, x1, x2, x3, w0, w1, w2, w3, sums_ref, near_ref, flip_ref, far_ref, farflip_ref,
    hidden, weight, starts, x_sems, w_sems, sems,
):
    copies, heads = [], []
    for i, ref in enumerate((w0, w1, w2, w3)):
        copies.append(pltpu.make_async_copy(ref, weight.at[i], w_sems.at[i]))
    for i, ref in enumerate((x0, x1, x2, x3)):
        for j in range(2):
            heads.append(
                pltpu.make_async_copy(ref.at[pl.ds(j * S, 16)], starts.at[i, j], sems.at[i, j])
            )
        copies.append(pltpu.make_async_copy(ref, hidden.at[i], x_sems.at[i]))
    for copy in heads + copies:
        copy.start()
    xs, ws = [hidden.at[i] for i in range(4)], [weight.at[i] for i in range(4)]
    there, back = (4 - y_ref[0]) % 4, y_ref[0]
    blocks = [(ws[m], z, (z * 4 + m) * 128) for z in range(2) for m in range(4)]

    def reduce(values, first):
        total = None
        for ref, z, at in blocks:
            term = mm(values[:, at : at + 128], ref[z, :, first : first + QUARTER])
            total = term if total is None else total + term
        return total

    def expand(values, first):
        return jnp.concatenate(
            [mm_nt(values, ref[z, :, first : first + QUARTER]) for ref, z, _ in blocks], 1
        )

    for copy in heads + copies[:4]:
        copy.wait()
    lead = jnp.concatenate([starts[i, j, :1] for i in range(4) for j in range(2)], 0).astype(F32)
    query = reduce(turn(lead, there).astype(BF16), 0).astype(BF16).astype(F32)
    head, col = iota((32, QUARTER), 0) // 8, iota((32, QUARTER), 1) // HD
    spread = jnp.where(head == col, jnp.concatenate([query] * 4, 0), 0.0).astype(BF16)
    keyed = turn(expand(spread, QUARTER), back).astype(BF16)
    logits = []
    for copy, x in zip(copies[4:], xs):
        copy.wait()
        logits.append(mm_nt(keyed, x[: 2 * S]))
    logits = jnp.concatenate(logits, 1) * HD ** (-0.5)
    live = jnp.concatenate([x[2 * S : 2 * S + 1, : 2 * S].astype(F32) for x in xs], 1)
    pair, slot = iota((32, 8 * S), 0) % 8, iota((32, 8 * S), 1) // S
    logits = jnp.where((pair == slot) & (live > 0.5), logits, -1e30)
    weights = jnp.exp(logits - jnp.max(logits, -1, keepdims=True))
    weights = (weights / jnp.sum(weights, -1, keepdims=True)).astype(BF16)
    mixed = mm(weights[:, : 2 * S], xs[0][: 2 * S])
    for i in range(1, 4):
        mixed += mm(weights[:, i * 2 * S : (i + 1) * 2 * S], xs[i][: 2 * S])
    context = reduce(turn(mixed, there).astype(BF16), 2 * QUARTER)
    context = jnp.where(head == col, context, 0.0)
    context = (context[:8] + context[8:16] + context[16:24] + context[24:]).astype(BF16)
    projected = turn(expand(context, 3 * QUARTER), back)
    own = projected[:2] + lead[:2]
    core, far, both = projected[2:4], projected[4:6], projected[6:]
    student = jnp.concatenate([sums_ref[0, 0:1, 48:49], sums_ref[0, 2:3, 48:49]], 0)
    student = jnp.broadcast_to(jnp.concatenate([student] * 4, 0), (8, 128))
    for ref, order in (
        (near_ref, (own, core, far, both)),
        (flip_ref, (core, own, both, far)),
        (far_ref, (far, both, own, core)),
        (farflip_ref, (both, far, core, own)),
    ):
        ref[:, :DT] = jnp.concatenate(order, 0)
        ref[:, DT:] = student


def teacher_partial(y, xs, ws, sums):
    shape = jax.ShapeDtypeStruct((8, DT + 128), F32)
    vmem = pl.BlockSpec(memory_space=pltpu.VMEM)
    return pl.pallas_call(
        teacher_kernel,
        out_shape=(shape,) * 4,
        in_specs=[pl.BlockSpec(memory_space=pltpu.SMEM)]
        + [pl.BlockSpec(memory_space=pl.ANY)] * 8
        + [vmem],
        out_specs=(vmem,) * 4,
        scratch_shapes=[
            pltpu.VMEM((4, 2 * S + 16, DT), BF16),
            pltpu.VMEM((4, 2, 128, DT), BF16),
            pltpu.VMEM((4, 2, 16, DT), BF16),
            pltpu.SemaphoreType.DMA((4,)),
            pltpu.SemaphoreType.DMA((4,)),
            pltpu.SemaphoreType.DMA((4, 2)),
        ],
        compiler_params=params(60),
        cost_estimate=pl.CostEstimate(flops=10**9, bytes_accessed=6 * 10**6, transcendentals=0),
        name="teacher_partial",
    )(y.reshape(1), *xs, *ws, sums)


def score_kernel(own, core, far, both, gain, weight, tile_ref, spread_ref, score_ref):
    refs = (own, core, far, both)
    values = own[:, :DT] + core[:, :DT] + far[:, :DT] + both[:, :DT]
    centred = values - jnp.mean(values, -1, keepdims=True)
    unit = centred * lax.rsqrt(jnp.mean(centred * centred, -1, keepdims=True) + EPS)
    score = jnp.sum(unit * gain[...] * weight[...], -1, keepdims=True)
    student = jnp.concatenate([ref[:2, DT:] for ref in refs], 0)
    tile = jnp.where(iota((8, 128), 1) < 64, score, student)
    tile_ref[...] = tile
    for i in range(2):
        score_ref[i] = jnp.sum(score[i : i + 1])
    for i in range(16):
        spread_ref[i] = tile


def score_tile(parts, gain, weight):
    vmem = pl.BlockSpec(memory_space=pltpu.VMEM)
    return pl.pallas_call(
        score_kernel,
        out_shape=(
            jax.ShapeDtypeStruct((8, 128), F32),
            jax.ShapeDtypeStruct((16, 8, 128), F32),
            jax.ShapeDtypeStruct((2,), F32),
        ),
        in_specs=[vmem] * 6,
        out_specs=(vmem, vmem, pl.BlockSpec(memory_space=pltpu.SMEM)),
        name="score_tile",
    )(*parts, gain, weight)


def payload_kernel(
    half_ref, tile_ref, all_ref, q_ref, p_ref, gp_hbm, recv_hbm, sums_ref, g_ref, out_hbm,
    gp, recv, out, gp_sems, recv_sems, out_sems,
):
    def block(ref, k):
        return ref.at[:, :, pl.ds(k * DS, DS)]

    def load_grad(k):
        return pltpu.make_async_copy(block(gp_hbm, k), block(gp, k), gp_sems.at[k])

    def load_term(k):
        return pltpu.make_async_copy(block(recv_hbm, k), block(recv, k), recv_sems.at[k])

    def save(k):
        cols = pl.ds(k * DS, DS) if k < 3 else pl.ds(WIDE, PAY - WIDE)
        return pltpu.make_async_copy(out.at[:, cols], out_hbm.at[:, cols], out_sems.at[k])

    load_grad(3).start()
    for k in range(3):
        load_grad(k).start()
        load_term(k).start()
    every = jnp.concatenate([all_ref[:, :4], all_ref[:, 4:]], 0)
    top = jnp.max(every, 0)
    lse = top + jnp.log(jnp.sum(jnp.exp(every - top[None]), 0))
    share = jnp.exp(tile_ref[:4] - lse)
    cot = LOSS_SCALE * (share[:, 64:65] - share[:, :1])
    wide = []
    for i in range(2):
        rows = jnp.concatenate([q_ref[i], p_ref[i]], 0)
        wide.append(select_features(half_ref[0], rows) * cot[i : i + 1])
    main = [values.astype(BF16) for values in wide]
    by_group = jnp.concatenate([cot[j : j + 1] for j in range(2) for _ in range(2)], 0)
    scaled = sums_ref[...] * by_group[None]
    high = scaled.astype(BF16).astype(F32)
    scaled = jnp.where(iota((CHIPS, 4, 128), 2) < 64, high, scaled - high)
    scaled = jnp.concatenate([scaled, scaled], 1).reshape(8 * CHIPS, 128)
    out[:, WIDE : WIDE + 128] = scaled.astype(BF16)
    grad = g_ref[...].astype(F32)
    grad = jnp.concatenate([grad[:, : DS // 2], grad[:, DS // 2 :]], 0)
    out[:, WIDE + 128 :] = jnp.concatenate([grad] * CHIPS, 0).astype(BF16)
    save(3).start()
    load_grad(3).wait()
    for k in range(3):
        rest = [late_features(values, k) for values in wide]
        load_grad(k).wait()
        load_term(k).wait()
        for part in range(3):
            cols = slice(k * DS + part * 256, k * DS + part * 256 + 256)
            late = slice(3 * DS + part * 256, 3 * DS + part * 256 + 256)
            total = mm(main[0], gp[0, :, cols])
            total += mm(main[1], gp[1, :, cols])
            total += mm(rest[0], gp[0, :, late])
            total += mm(rest[1], gp[1, :, late])
            for i in range(2):
                total += recv[i, :, cols].astype(F32) * cot[2 + i : 3 + i]
            out[:, cols] = total.astype(BF16)
        save(k).start()
    for k in range(4):
        save(k).wait()


def payload(half, tile, every, own_query, passages, grad_pre, received, sums, grad):
    vmem = pl.BlockSpec(memory_space=pltpu.VMEM)
    anywhere = pl.BlockSpec(memory_space=pl.ANY)
    return pl.pallas_call(
        payload_kernel,
        out_shape=jax.ShapeDtypeStruct((CHIPS * 8, PAY), BF16),
        in_specs=[pl.BlockSpec(memory_space=pltpu.SMEM)]
        + [vmem] * 4
        + [anywhere, anywhere, vmem, vmem],
        out_specs=anywhere,
        scratch_shapes=[
            pltpu.VMEM((2, S, FF), BF16),
            pltpu.VMEM((2, 8 * CHIPS, WIDE), BF16),
            pltpu.VMEM((8 * CHIPS, PAY), BF16),
            pltpu.SemaphoreType.DMA((4,)),
            pltpu.SemaphoreType.DMA((3,)),
            pltpu.SemaphoreType.DMA((4,)),
        ],
        compiler_params=params(60),
        name="payload",
    )(half.reshape(1), tile, every, own_query, passages, grad_pre, received, sums, grad)


def final_kernel(core_ref, in_ref, gin_ref, own_ref, send_ref):
    total = in_ref[0, :, :WIDE].astype(F32)
    for d in range(1, CHIPS):
        total += in_ref[d, :, :WIDE].astype(F32)
    gin_ref[:, :WIDE] = total[:6]
    for r in range(6):
        line, at = 6 + r // 3, r % 3 * DS
        gin_ref[r : r + 1, WIDE:] = total[line : line + 1, at : at + DS]
    columns = in_ref[:, :, WIDE : WIDE + 128].astype(F32).reshape(CHIPS * 8, 128).T
    line = iota((128, CHIPS * 8), 1) % 8
    grads = in_ref[:, :, WIDE + 128 :].astype(F32).reshape(CHIPS * 8, DS // 2).astype(BF16)
    left = mm(jnp.where(line < 4, columns, 0.0).astype(BF16), grads)
    right = mm(jnp.where(line < 4, 0.0, columns).astype(BF16), grads)
    both = jnp.concatenate([left[:48] + left[64:112], right[:48] + right[64:112]], 1)
    first = core_ref[0] == 0
    own_ref[...] = jnp.where(first, both[:24], both[24:])
    send_ref[...] = jnp.where(first, both[24:], both[:24])


def final(core, incoming):
    vmem = pl.BlockSpec(memory_space=pltpu.VMEM)
    part = jax.ShapeDtypeStruct((24, DS), F32)
    return pl.pallas_call(
        final_kernel,
        out_shape=(jax.ShapeDtypeStruct((6, FF), F32), part, part),
        in_specs=[pl.BlockSpec(memory_space=pltpu.SMEM), vmem],
        out_specs=(vmem,) * 3,
        compiler_params=params(32),
        name="final",
    )(core.reshape(1), incoming)


def exchange_weights(qkv_weight, out_weight):
    zl, core = lax.axis_index("zl"), lax.axis_index("c")
    me = 2 * zl + core
    heads = qkv_weight.reshape(16, 3, 4, QUARTER).transpose(2, 0, 1, 3).reshape(4, 16, 3 * QUARTER)
    outs = out_weight.T.reshape(16, 4, QUARTER).transpose(1, 0, 2)
    packed = jnp.concatenate([heads, outs], -1)
    pick = lambda index: lax.dynamic_index_in_dim(packed, index, 0, keepdims=True)
    mine = pick(me)
    from_core = lax.ppermute(pick(me ^ 1), "c", SWAP)
    from_far = lax.ppermute(pick(me ^ 2), "zl", SWAP)
    from_both = lax.ppermute(pick(me ^ 3), ("zl", "c"), BOTH)
    four = jnp.zeros((4, 16, DT), BF16)
    for part, who in ((mine, me), (from_core, me ^ 1), (from_far, me ^ 2), (from_both, me ^ 3)):
        four = lax.dynamic_update_slice(four, part, (who, 0, 0))
    return four.reshape(2, 1, 1, 32, DT)


def body(
    teacher_hidden,
    passage_len,
    qkv_weight,
    out_weight,
    teacher_gain,
    score_weight,
    query_tokens,
    passage_tokens,
    w_in,
    w_out,
):
    core = lax.axis_index("c")
    first = lax.axis_index("xl") * 4 + core * 2

    slots = jnp.arange(S)
    live = (slots[None, :] < SQ) | (slots[None, :] - SQ < passage_len[:, None])
    live = jnp.pad(live.astype(BF16).reshape(1, 2 * S), ((0, 15), (0, DT - 2 * S)))
    hidden = jnp.concatenate([teacher_hidden.reshape(2 * S, DT), live], 0)
    own_query = lax.dynamic_slice_in_dim(query_tokens, first, 2, 0)

    four = exchange_weights(qkv_weight, out_weight)
    four, hidden = lax.optimization_barrier((four, hidden))
    hidden_far = lax.ppermute(hidden, "zl", SWAP)
    hidden_core = lax.ppermute(hidden, "c", SWAP)
    plane = join_axis(send_axis(four, X), X, 2)
    plane, own_query, hidden_core = lax.optimization_barrier((plane, own_query, hidden_core))
    planes = send_axis(plane, "y")

    scalars = jnp.concatenate([passage_len, 1 - core.reshape(1)])
    sums, grad, grad_pre, other = student(scalars, own_query, passage_tokens, w_in, w_out)

    planes, other, hidden_far = lax.optimization_barrier((planes, other, hidden_far))
    hidden_both = lax.ppermute(hidden_far, "c", SWAP)
    here, before, after, across = [part.reshape(2, 128, DT) for part in planes]
    near, flip, far, farflip = teacher_partial(
        lax.axis_index("y"),
        (hidden, hidden_core, hidden_far, hidden_both),
        (here, after, across, before),
        sums,
    )
    parts = (
        near,
        lax.ppermute(flip, "c", SWAP),
        lax.ppermute(far, "zl", SWAP),
        lax.ppermute(farflip, ("zl", "c"), BOTH),
    )
    other, _ = lax.optimization_barrier((other, near))
    received = lax.ppermute(other, "c", SWAP)
    tile, spread, scores = score_tile(parts, teacher_gain[None], score_weight[None])
    every = lax.all_to_all(spread, RIVALS, 0, 0, tiled=True)
    outgoing = payload(
        core, tile, every, own_query, passage_tokens, grad_pre, received, sums, grad
    )
    incoming = lax.all_to_all(outgoing.reshape(CHIPS, 8, PAY), CHIP_AXES, 0, 0, tiled=True)
    grad_in, own_out, send_out = final(core, incoming)
    return (scores, grad_in, own_out + lax.ppermute(send_out, "c", SWAP))


def solution(mesh):
    fine = Mesh(mesh.devices.reshape(2, 2, 4, 2, 2, 2), AXES)
    placed = (
        P(AXES, None, None),
        P(AXES),
        P(DP, None),
        P(None, DP),
        P(),
        P(),
        P(),
        P(AXES, None, None),
        P(),
        P(),
    )
    return jax.shard_map(
        body,
        mesh=fine,
        in_specs=placed,
        out_specs=(P(AXES), P(AXES, None), P(AXES, None)),
        check_vma=False,
    )
```

```python
import jax
import jax.numpy as jnp
from jax import lax
from jax.experimental import pallas as pl
from jax.experimental.pallas import tpu as pltpu
from jax.sharding import Mesh
from jax.sharding import PartitionSpec as P

HD = 64
SQ = 32
SP = 224
S = SQ + SP
DT = 1024
DS = 768
FF = 3072
CHIPS = 64
QUARTER = 4 * HD
WIDE = 3 * DS
PAY = WIDE + 128 + DS // 2
EPS = 1e-05
LOSS_SCALE = 8.0
MIB = 1 << 20

AXES = ("zh", "zl", "y", "xh", "xl", "c")
DP = ("zl", "y", "xh", "xl", "c")
X = ("xh", "xl")
CHIP_AXES = ("zh", "zl", "y", "xh", "xl")
RIVALS = ("zh", "y", "xh")
SWAP = [(0, 1), (1, 0)]
BOTH = [(0, 3), (1, 2), (2, 1), (3, 0)]

F32 = jnp.float32
BF16 = jnp.bfloat16
NT = (((1,), (1,)), ((), ()))


def params(mib):
    return pltpu.CompilerParams(vmem_limit_bytes=mib * MIB)


def ring(step):
    return [(i, (i + step) % 4) for i in range(4)]


def mm(a, b):
    return jnp.dot(a, b, preferred_element_type=F32)


def mm_nt(a, b):
    return lax.dot_general(a, b, NT, preferred_element_type=F32)


def iota(shape, dim):
    return lax.broadcasted_iota(jnp.int32, shape, dim)


def send_axis(piece, axis):
    return [piece] + [lax.ppermute(piece, axis, ring(step)) for step in (1, 3, 2)]


def join_axis(pieces, axis, dim):
    here, piece = lax.axis_index(axis), pieces[0]
    shape = piece.shape[:dim] + (4,) + piece.shape[dim + 1 :]
    whole = jnp.zeros(shape, piece.dtype)
    for part, step in zip(pieces, (0, 1, 3, 2)):
        start = [0] * len(shape)
        start[dim] = (here - step) % 4
        whole = lax.dynamic_update_slice(whole, part, tuple(start))
    return whole


def student_kernel(
    lens, half_ref, q_ref, p_ref, win_hbm, wout_hbm, sums_tiles, score_ref, g_ref, gp_hbm, other_hbm,
    rows, win, wout, slope, pulled_ref, sums_ref, gp, blocks, in_sems, out_sems, wout_sem, other_sems,
):
    def load(j):
        cols = pl.ds(pl.multiple_of(j * 512, 512), 512)
        return pltpu.make_async_copy(win_hbm.at[:, cols], win.at[:, cols], in_sems.at[j])

    def save(j):
        cols = pl.ds(pl.multiple_of(j * DS, DS), DS)
        return pltpu.make_async_copy(gp.at[:, :, cols], gp_hbm.at[:, :, cols], out_sems.at[j])

    def send(i, k):
        cols = pl.ds(k * DS, DS)
        return pltpu.make_async_copy(
            blocks.at[i, :, cols], other_hbm.at[i, :, cols], other_sems.at[i * 3 + k]
        )

    load_out = pltpu.make_async_copy(wout_hbm, wout, wout_sem)
    for j in range(6):
        load(j).start()
    load_out.start()
    for i in range(2):
        rows[i * S : i * S + SQ] = q_ref[i]
        rows[i * S + SQ : (i + 1) * S] = p_ref[i]
    at_row = iota((S, 1), 0) - SQ

    def pool(values):
        sums = []
        for i in range(2):
            part = values[i * S : (i + 1) * S].astype(F32)
            sums.append(jnp.sum(part[:SQ], 0, keepdims=True))
            part = jnp.where(at_row[SQ:] < lens[i], part[SQ:], 0.0)
            sums.append(jnp.sum(part, 0, keepdims=True))
        return jnp.concatenate(sums + sums, 0)


    def forward(j, carry):
        load(j).wait()
        for part in range(2):
            cols = pl.ds(pl.multiple_of(j * 512 + part * 256, 256), 256)
            pre = mm(rows[...], win[:, cols])
            bell = jnp.exp2(pre * pre * -0.7213475204444817)
            denominator = 1.0 + jnp.abs(pre) * (0.3275911 * 0.7071067811865476)
            t = pl.reciprocal(denominator, approx=True)
            t = t * (2.0 - denominator * t)
            poly = 0.5 * 1.061405429 * t - 0.5 * 1.453152027
            poly = poly * t + 0.5 * 1.421413741
            poly = poly * t - 0.5 * 0.284496736
            poly = poly * t + 0.5 * 0.254829592
            tail = poly * t * bell
            cdf = jnp.where(pre < 0.0, tail, 1.0 - tail)
            slope[:, cols] = cdf + pre * bell * 0.3989422804014327
            sums_ref[:, cols] = pool(pre * cdf)
        return carry

    lax.fori_loop(0, FF // 512, forward, 0)
    load_out.wait()
    sums = sums_ref[...]
    high = sums.astype(BF16)
    low = (sums - high.astype(F32)).astype(BF16)
    out = mm(jnp.concatenate([high, low], 0), wout[...])
    row8 = iota((8, 1), 0)
    count = jnp.where(row8 % 2 == 0, SQ, jnp.where(row8 < 2, lens[0], lens[1])).astype(F32)
    means = (pool(rows[...]) + out[:8] + out[8:]) / count
    means = means[:4]
    centred = means - jnp.mean(means, -1, keepdims=True)
    scale = lax.rsqrt(jnp.mean(centred * centred, -1, keepdims=True) + EPS)
    unit = centred * scale
    other = jnp.concatenate([unit[1:2], unit[0:1], unit[3:4], unit[2:3]], 0)
    cross = jnp.sum(unit * other, -1, keepdims=True) * DS ** (-0.5)
    back = other * DS ** (-0.5)
    back = scale * (
        back
        - jnp.mean(back, -1, keepdims=True)
        - unit * jnp.mean(back * unit, -1, keepdims=True)
    )
    grad = (back / count[:4]).astype(BF16)
    g_ref[...] = grad
    pairs = jnp.concatenate([cross[0:1], cross[2:3]], 0)
    score_ref[...] = jnp.broadcast_to(jnp.concatenate([pairs] * 4, 0), (8, 128))
    grad8 = jnp.concatenate([grad, jnp.zeros((4, DS), BF16)], 0)
    pulled_ref[...] = mm_nt(grad8, wout[...])
    def backward(j, carry):
        for part in range(3):
            cols = pl.ds(pl.multiple_of(j * DS + part * 256, 256), 256)
            pulled = pulled_ref[:, cols]
            for i in range(2):
                gate = jnp.where(at_row < lens[i], pulled[2 * i + 1 : 2 * i + 2], 0.0)
                gp[i, SQ:, cols] = (gate[SQ:] * slope[i * S + SQ : (i + 1) * S, cols]).astype(BF16)
                gp[i, :SQ, cols] = (
                    pulled[2 * i : 2 * i + 1] * slope[i * S : i * S + SQ, cols]
                ).astype(BF16)
        save(j).start()
        return carry

    lax.fori_loop(0, FF // DS, backward, 0)
    fill = jnp.zeros((4, 16), F32)
    for d in range(CHIPS):
        part = sums[:4, d * 48 : d * 48 + 48]
        sums_tiles[d] = jnp.concatenate([part, fill, part, fill], 1)
    grad_blocks(
        half_ref[0], rows, gp, blocks, lambda i, k: send(i, k).start()
    )
    for j in range(FF // DS):
        save(j).wait()
    for j in range(6):
        send(j // 3, j % 3).wait()


def student(lens, half, own_query, passages, w_in, w_out):
    vmem = pl.BlockSpec(memory_space=pltpu.VMEM)
    anywhere = pl.BlockSpec(memory_space=pl.ANY)
    return pl.pallas_call(
        student_kernel,
        out_shape=(
            jax.ShapeDtypeStruct((CHIPS, 4, 128), F32),
            jax.ShapeDtypeStruct((8, 128), F32),
            jax.ShapeDtypeStruct((4, DS), BF16),
            jax.ShapeDtypeStruct((2, S, FF), BF16),
            jax.ShapeDtypeStruct((2, 8 * CHIPS, WIDE), BF16),
        ),
        in_specs=[pl.BlockSpec(memory_space=pltpu.SMEM)] * 2 + [vmem, vmem, anywhere, anywhere],
        out_specs=(vmem, vmem, vmem, anywhere, anywhere),
        scratch_shapes=[
            pltpu.VMEM((2 * S, DS), BF16),
            pltpu.VMEM((DS, FF), BF16),
            pltpu.VMEM((FF, DS), BF16),
            pltpu.VMEM((2 * S, FF), F32),
            pltpu.VMEM((8, FF), F32),
            pltpu.VMEM((8, FF), F32),
            pltpu.VMEM((2, S, FF), BF16),
            pltpu.VMEM((2, 8 * CHIPS, WIDE), BF16),
            pltpu.SemaphoreType.DMA((6,)),
            pltpu.SemaphoreType.DMA((4,)),
            pltpu.SemaphoreType.DMA,
            pltpu.SemaphoreType.DMA((6,)),
        ],
        compiler_params=params(60),
        cost_estimate=pl.CostEstimate(flops=1, bytes_accessed=1, transcendentals=0),
        name="student",
    )(lens, half.reshape(1), own_query, passages, w_in, w_out)


def select_features(half, rows):
    line, feature = iota((8 * CHIPS, DS), 0), iota((8 * CHIPS, DS), 1)
    lane = line % 8
    wanted = jnp.where(lane < 6, (2 * (line // 8) + half) * 6 + lane, -1)
    return mm_nt(jnp.where(feature == wanted, 1.0, 0.0).astype(BF16), rows)


def late_features(wide, k):
    lane = iota((8 * CHIPS, S), 0) % 8
    return jnp.where(
        lane == 6,
        pltpu.roll(wide, 6 - k, 0),
        jnp.where(lane == 7, pltpu.roll(wide, 4 - k, 0), 0.0),
    ).astype(BF16)


def grad_blocks(half, rows, grad, out, done):
    for i in range(2):
        wide = select_features(half, rows[i * S : (i + 1) * S])
        main = wide.astype(BF16)
        for k in range(3):
            rest = late_features(wide, k)
            for part in range(3):
                at = k * DS + part * 256
                late = 3 * DS + part * 256
                out[i, :, at : at + 256] = (
                    mm(main, grad[i, :, at : at + 256]) + mm(rest, grad[i, :, late : late + 256])
                ).astype(BF16)
            done(i, k)


def first_kernel(half_ref, q_ref, p_ref, gp_hbm, out_hbm, gp, out, gp_sems, out_sems):
    def block(ref, k):
        return ref.at[:, pl.ds(k * DS, DS)]

    def load(k):
        return pltpu.make_async_copy(block(gp_hbm.at[0], k), block(gp, k), gp_sems.at[k])

    def save(k):
        return pltpu.make_async_copy(block(out, k), block(out_hbm, k), out_sems.at[k])

    for k in (3, 0, 1, 2):
        load(k).start()
    wide = select_features(half_ref[0], jnp.concatenate([q_ref[0], p_ref[0]], 0))
    main = wide.astype(BF16)
    load(3).wait()
    for k in range(3):
        rest = late_features(wide, k)
        load(k).wait()
        for part in range(3):
            cols = slice(k * DS + part * 256, k * DS + part * 256 + 256)
            late = slice(3 * DS + part * 256, 3 * DS + part * 256 + 256)
            out[:, cols] = (mm(main, gp[:, cols]) + mm(rest, gp[:, late])).astype(BF16)
        save(k).start()
    for k in range(3):
        save(k).wait()


def first_term(half, own_query, passages, grad_pre):
    vmem = pl.BlockSpec(memory_space=pltpu.VMEM)
    anywhere = pl.BlockSpec(memory_space=pl.ANY)
    return pl.pallas_call(
        first_kernel,
        out_shape=jax.ShapeDtypeStruct((8 * CHIPS, WIDE), BF16),
        in_specs=[pl.BlockSpec(memory_space=pltpu.SMEM), vmem, vmem, anywhere],
        out_specs=anywhere,
        scratch_shapes=[
            pltpu.VMEM((S, FF), BF16),
            pltpu.VMEM((8 * CHIPS, WIDE), BF16),
            pltpu.SemaphoreType.DMA((4,)),
            pltpu.SemaphoreType.DMA((3,)),
        ],
        compiler_params=params(60),
        cost_estimate=pl.CostEstimate(flops=3 * 10**9, bytes_accessed=4 * 10**6, transcendentals=0),
        name="first_term",
    )(half.reshape(1), own_query, passages, grad_pre)


def turn(values, shift):
    wide = values.shape[1] // 2
    amount = shift * 128
    return jnp.concatenate(
        [pltpu.roll(values[:, :wide], amount, 1), pltpu.roll(values[:, wide:], amount, 1)], 1
    )


def teacher_kernel(
    y_ref, x0, x1, x2, x3, w0, w1, w2, w3, student_ref, near_ref, flip_ref, far_ref, farflip_ref,
    hidden, weight, starts, x_sems, w_sems, sems,
):
    copies, heads = [], []
    for i, ref in enumerate((w0, w1, w2, w3)):
        copies.append(pltpu.make_async_copy(ref, weight.at[i], w_sems.at[i]))
    for i, ref in enumerate((x0, x1, x2, x3)):
        for j in range(2):
            heads.append(
                pltpu.make_async_copy(ref.at[pl.ds(j * S, 16)], starts.at[i, j], sems.at[i, j])
            )
        copies.append(pltpu.make_async_copy(ref, hidden.at[i], x_sems.at[i]))
    for copy in heads + copies:
        copy.start()
    xs, ws = [hidden.at[i] for i in range(4)], [weight.at[i] for i in range(4)]
    there, back = (4 - y_ref[0]) % 4, y_ref[0]
    blocks = [(ws[m], z, (z * 4 + m) * 128) for z in range(2) for m in range(4)]

    def reduce(values, first):
        total = None
        for ref, z, at in blocks:
            term = mm(values[:, at : at + 128], ref[z, :, first : first + QUARTER])
            total = term if total is None else total + term
        return total

    def expand(values, first):
        return jnp.concatenate(
            [mm_nt(values, ref[z, :, first : first + QUARTER]) for ref, z, _ in blocks], 1
        )

    for copy in heads + copies[:4]:
        copy.wait()
    lead = jnp.concatenate([starts[i, j, :1] for i in range(4) for j in range(2)], 0).astype(F32)
    query = reduce(turn(lead, there).astype(BF16), 0).astype(BF16).astype(F32)
    head, col = iota((32, QUARTER), 0) // 8, iota((32, QUARTER), 1) // HD
    spread = jnp.where(head == col, jnp.concatenate([query] * 4, 0), 0.0).astype(BF16)
    keyed = turn(expand(spread, QUARTER), back).astype(BF16)
    logits = []
    for copy, x in zip(copies[4:], xs):
        copy.wait()
        logits.append(mm_nt(keyed, x[: 2 * S]))
    logits = jnp.concatenate(logits, 1) * HD ** (-0.5)
    live = jnp.concatenate([x[2 * S : 2 * S + 1, : 2 * S].astype(F32) for x in xs], 1)
    pair, slot = iota((32, 8 * S), 0) % 8, iota((32, 8 * S), 1) // S
    logits = jnp.where((pair == slot) & (live > 0.5), logits, -1e30)
    weights = jnp.exp(logits - jnp.max(logits, -1, keepdims=True))
    weights = (weights / jnp.sum(weights, -1, keepdims=True)).astype(BF16)
    mixed = mm(weights[:, : 2 * S], xs[0][: 2 * S])
    for i in range(1, 4):
        mixed += mm(weights[:, i * 2 * S : (i + 1) * 2 * S], xs[i][: 2 * S])
    context = reduce(turn(mixed, there).astype(BF16), 2 * QUARTER)
    context = jnp.where(head == col, context, 0.0)
    context = (context[:8] + context[8:16] + context[16:24] + context[24:]).astype(BF16)
    projected = turn(expand(context, 3 * QUARTER), back)
    own = projected[:2] + lead[:2]
    core, far, both = projected[2:4], projected[4:6], projected[6:]
    for ref, order in (
        (near_ref, (own, core, far, both)),
        (flip_ref, (core, own, both, far)),
        (far_ref, (far, both, own, core)),
        (farflip_ref, (both, far, core, own)),
    ):
        ref[:, :DT] = jnp.concatenate(order, 0)
        ref[:, DT:] = student_ref[...]


def teacher_partial(y, xs, ws, student_scores):
    shape = jax.ShapeDtypeStruct((8, DT + 128), F32)
    vmem = pl.BlockSpec(memory_space=pltpu.VMEM)
    return pl.pallas_call(
        teacher_kernel,
        out_shape=(shape,) * 4,
        in_specs=[pl.BlockSpec(memory_space=pltpu.SMEM)]
        + [pl.BlockSpec(memory_space=pl.ANY)] * 8
        + [vmem],
        out_specs=(vmem,) * 4,
        scratch_shapes=[
            pltpu.VMEM((4, 2 * S + 16, DT), BF16),
            pltpu.VMEM((4, 2, 128, DT), BF16),
            pltpu.VMEM((4, 2, 16, DT), BF16),
            pltpu.SemaphoreType.DMA((4,)),
            pltpu.SemaphoreType.DMA((4,)),
            pltpu.SemaphoreType.DMA((4, 2)),
        ],
        compiler_params=params(24),
        cost_estimate=pl.CostEstimate(flops=10**9, bytes_accessed=6 * 10**6, transcendentals=0),
        name="teacher_partial",
    )(y.reshape(1), *xs, *ws, student_scores)


def score_kernel(own, core, far, both, gain, weight, tile_ref, spread_ref, score_ref):
    refs = (own, core, far, both)
    values = own[:, :DT] + core[:, :DT] + far[:, :DT] + both[:, :DT]
    centred = values - jnp.mean(values, -1, keepdims=True)
    unit = centred * lax.rsqrt(jnp.mean(centred * centred, -1, keepdims=True) + EPS)
    score = jnp.sum(unit * gain[...] * weight[...], -1, keepdims=True)
    student = jnp.concatenate([ref[:2, DT:] for ref in refs], 0)
    tile = jnp.where(iota((8, 128), 1) < 64, score, student)
    tile_ref[...] = tile
    for i in range(2):
        score_ref[i] = jnp.sum(score[i : i + 1])
    for i in range(16):
        spread_ref[i] = tile


def score_tile(parts, gain, weight):
    vmem = pl.BlockSpec(memory_space=pltpu.VMEM)
    return pl.pallas_call(
        score_kernel,
        out_shape=(
            jax.ShapeDtypeStruct((8, 128), F32),
            jax.ShapeDtypeStruct((16, 8, 128), F32),
            jax.ShapeDtypeStruct((2,), F32),
        ),
        in_specs=[vmem] * 6,
        out_specs=(vmem, vmem, pl.BlockSpec(memory_space=pltpu.SMEM)),
        compiler_params=params(8),
        name="score_tile",
    )(*parts, gain, weight)


def payload_kernel(
    half_ref, tile_ref, all_ref, q_ref, p_ref, gp_hbm, first_hbm, recv_hbm, sums_ref, g_ref, out_hbm,
    gp, term, recv, out, gp_sems, term_sems, recv_sems, out_sems,
):
    def load_grad(k):
        cols = pl.ds(k * DS, DS)
        return pltpu.make_async_copy(gp_hbm.at[1, :, cols], gp.at[:, cols], gp_sems.at[k])

    def load_first(k):
        cols = pl.ds(k * DS, DS)
        return pltpu.make_async_copy(first_hbm.at[:, cols], term.at[:, cols], term_sems.at[k])

    def load_term(k):
        cols = pl.ds(k * DS, DS)
        return pltpu.make_async_copy(recv_hbm.at[:, :, cols], recv.at[:, :, cols], recv_sems.at[k])

    def save(k):
        cols = pl.ds(k * DS, DS) if k < 3 else pl.ds(WIDE, PAY - WIDE)
        return pltpu.make_async_copy(out.at[:, cols], out_hbm.at[:, cols], out_sems.at[k])

    load_grad(3).start()
    for k in range(3):
        load_grad(k).start()
        load_first(k).start()
        load_term(k).start()
    every = jnp.concatenate([all_ref[:, :4], all_ref[:, 4:]], 0)
    top = jnp.max(every, 0)
    lse = top + jnp.log(jnp.sum(jnp.exp(every - top[None]), 0))
    share = jnp.exp(tile_ref[:4] - lse)
    cot = LOSS_SCALE * (share[:, 64:65] - share[:, :1])
    rows = jnp.concatenate([q_ref[1], p_ref[1]], 0)
    wide = select_features(half_ref[0], rows) * cot[1:2]
    main = wide.astype(BF16)
    by_group = jnp.concatenate([cot[j : j + 1] for j in range(2) for _ in range(2)], 0)
    scaled = sums_ref[...] * by_group[None]
    high = scaled.astype(BF16).astype(F32)
    scaled = jnp.where(iota((CHIPS, 4, 128), 2) < 64, high, scaled - high)
    scaled = jnp.concatenate([scaled, scaled], 1).reshape(8 * CHIPS, 128)
    out[:, WIDE : WIDE + 128] = scaled.astype(BF16)
    grad = g_ref[...].astype(F32)
    grad = jnp.concatenate([grad[:, : DS // 2], grad[:, DS // 2 :]], 0)
    out[:, WIDE + 128 :] = jnp.concatenate([grad] * CHIPS, 0).astype(BF16)
    save(3).start()
    load_grad(3).wait()
    for k in range(3):
        rest = late_features(wide, k)
        load_grad(k).wait()
        load_first(k).wait()
        load_term(k).wait()
        for part in range(3):
            cols = slice(k * DS + part * 256, k * DS + part * 256 + 256)
            late = slice(3 * DS + part * 256, 3 * DS + part * 256 + 256)
            total = mm(main, gp[:, cols]) + mm(rest, gp[:, late])
            total += term[:, cols].astype(F32) * cot[:1]
            for i in range(2):
                total += recv[i, :, cols].astype(F32) * cot[2 + i : 3 + i]
            out[:, cols] = total.astype(BF16)
        save(k).start()
    for k in range(4):
        save(k).wait()


def payload(half, tile, every, own_query, passages, grad_pre, first, received, sums, grad):
    vmem = pl.BlockSpec(memory_space=pltpu.VMEM)
    anywhere = pl.BlockSpec(memory_space=pl.ANY)
    return pl.pallas_call(
        payload_kernel,
        out_shape=jax.ShapeDtypeStruct((CHIPS * 8, PAY), BF16),
        in_specs=[pl.BlockSpec(memory_space=pltpu.SMEM)]
        + [vmem] * 4
        + [anywhere, anywhere, anywhere, vmem, vmem],
        out_specs=anywhere,
        scratch_shapes=[
            pltpu.VMEM((S, FF), BF16),
            pltpu.VMEM((8 * CHIPS, WIDE), BF16),
            pltpu.VMEM((2, 8 * CHIPS, WIDE), BF16),
            pltpu.VMEM((8 * CHIPS, PAY), BF16),
            pltpu.SemaphoreType.DMA((4,)),
            pltpu.SemaphoreType.DMA((3,)),
            pltpu.SemaphoreType.DMA((3,)),
            pltpu.SemaphoreType.DMA((4,)),
        ],
        compiler_params=params(60),
        name="payload",
    )(half.reshape(1), tile, every, own_query, passages, grad_pre, first, received, sums, grad)


def final_kernel(core_ref, in_ref, gin_ref, own_ref, send_ref):
    total = in_ref[0, :, :WIDE].astype(F32)
    for d in range(1, CHIPS):
        total += in_ref[d, :, :WIDE].astype(F32)
    gin_ref[:, :WIDE] = total[:6]
    for r in range(6):
        line, at = 6 + r // 3, r % 3 * DS
        gin_ref[r : r + 1, WIDE:] = total[line : line + 1, at : at + DS]
    columns = in_ref[:, :, WIDE : WIDE + 128].astype(F32).reshape(CHIPS * 8, 128).T
    line = iota((128, CHIPS * 8), 1) % 8
    grads = in_ref[:, :, WIDE + 128 :].astype(F32).reshape(CHIPS * 8, DS // 2).astype(BF16)
    left = mm(jnp.where(line < 4, columns, 0.0).astype(BF16), grads)
    right = mm(jnp.where(line < 4, 0.0, columns).astype(BF16), grads)
    both = jnp.concatenate([left[:48] + left[64:112], right[:48] + right[64:112]], 1)
    first = core_ref[0] == 0
    own_ref[...] = jnp.where(first, both[:24], both[24:])
    send_ref[...] = jnp.where(first, both[24:], both[:24])


def final(core, incoming):
    vmem = pl.BlockSpec(memory_space=pltpu.VMEM)
    part = jax.ShapeDtypeStruct((24, DS), F32)
    return pl.pallas_call(
        final_kernel,
        out_shape=(jax.ShapeDtypeStruct((6, FF), F32), part, part),
        in_specs=[pl.BlockSpec(memory_space=pltpu.SMEM), vmem],
        out_specs=(vmem,) * 3,
        compiler_params=params(32),
        name="final",
    )(core.reshape(1), incoming)


def pack_kernel(me_ref, qkv_ref, out_ref, p0, p1, p2, p3):
    for flip, ref in enumerate((p0, p1, p2, p3)):
        for j in range(4):

            @pl.when(me_ref[0] == j)
            def _():
                who = j ^ flip
                for t in range(3):
                    at = t * DT + who * QUARTER
                    ref[0, :, t * QUARTER : (t + 1) * QUARTER] = qkv_ref[:, at : at + QUARTER]
                ref[0, :, 3 * QUARTER :] = out_ref[:, who * QUARTER : (who + 1) * QUARTER]


def pack_weights(me, qkv_weight, out_weight):
    vmem = pl.BlockSpec(memory_space=pltpu.VMEM)
    return pl.pallas_call(
        pack_kernel,
        out_shape=(jax.ShapeDtypeStruct((1, 16, DT), BF16),) * 4,
        in_specs=[pl.BlockSpec(memory_space=pltpu.SMEM), vmem, vmem],
        out_specs=(vmem,) * 4,
        compiler_params=params(8),
        name="pack_weights",
    )(me.reshape(1), qkv_weight, out_weight.T)


def exchange_weights(qkv_weight, out_weight):
    me = 2 * lax.axis_index("zl") + lax.axis_index("c")
    mine, to_core, to_far, to_both = pack_weights(me, qkv_weight, out_weight)
    from_core = lax.ppermute(to_core, "c", SWAP)
    from_far = lax.ppermute(to_far, "zl", SWAP)
    from_both = lax.ppermute(to_both, ("zl", "c"), BOTH)
    four = jnp.zeros((4, 16, DT), BF16)
    for part, who in ((mine, me), (from_core, me ^ 1), (from_far, me ^ 2), (from_both, me ^ 3)):
        four = lax.dynamic_update_slice(four, part, (who, 0, 0))
    return four.reshape(2, 1, 1, 32, DT)


def body(
    teacher_hidden,
    passage_len,
    qkv_weight,
    out_weight,
    teacher_gain,
    score_weight,
    query_tokens,
    passage_tokens,
    w_in,
    w_out,
):
    core = lax.axis_index("c")
    first = lax.axis_index("xl") * 4 + core * 2

    slots = jnp.arange(S)
    live = (slots[None, :] < SQ) | (slots[None, :] - SQ < passage_len[:, None])
    live = jnp.pad(live.astype(BF16).reshape(1, 2 * S), ((0, 15), (0, DT - 2 * S)))
    hidden = jnp.concatenate([teacher_hidden.reshape(2 * S, DT), live], 0)
    own_query = lax.dynamic_slice_in_dim(query_tokens, first, 2, 0)

    four = exchange_weights(qkv_weight, out_weight)
    four, hidden = lax.optimization_barrier((four, hidden))
    hidden_far = lax.ppermute(hidden, "zl", SWAP)
    hidden_core = lax.ppermute(hidden, "c", SWAP)
    plane = join_axis(send_axis(four, X), X, 2)
    plane, own_query, hidden_core = lax.optimization_barrier((plane, own_query, hidden_core))
    planes = send_axis(plane, "y")

    sums, student_scores, grad, grad_pre, other = student(
        passage_len, 1 - core, own_query, passage_tokens, w_in, w_out
    )

    planes, other, hidden_far = lax.optimization_barrier((planes, other, hidden_far))
    hidden_both = lax.ppermute(hidden_far, "c", SWAP)
    here, before, after, across = [part.reshape(2, 128, DT) for part in planes]
    near, flip, far, farflip = teacher_partial(
        lax.axis_index("y"),
        (hidden, hidden_core, hidden_far, hidden_both),
        (here, after, across, before),
        student_scores,
    )
    parts = (
        near,
        lax.ppermute(flip, "c", SWAP),
        lax.ppermute(far, "zl", SWAP),
        lax.ppermute(farflip, ("zl", "c"), BOTH),
    )
    tile, spread, scores = score_tile(parts, teacher_gain[None], score_weight[None])
    every = lax.all_to_all(spread, RIVALS, 0, 0, tiled=True)
    other, late_query, _ = lax.optimization_barrier((other, own_query, tile))
    received = lax.ppermute(other, "c", SWAP)
    term = first_term(core, late_query, passage_tokens, grad_pre)
    outgoing = payload(
        core, tile, every, own_query, passage_tokens, grad_pre, term, received, sums, grad
    )
    incoming = lax.all_to_all(outgoing.reshape(CHIPS, 8, PAY), CHIP_AXES, 0, 0, tiled=True)
    grad_in, own_out, send_out = final(core, incoming)
    return (scores, grad_in, own_out + lax.ppermute(send_out, "c", SWAP))


def solution(mesh):
    fine = Mesh(mesh.devices.reshape(2, 2, 4, 2, 2, 2), AXES)
    placed = (
        P(AXES, None, None),
        P(AXES),
        P(DP, None),
        P(None, DP),
        P(),
        P(),
        P(),
        P(AXES, None, None),
        P(),
        P(),
    )
    return jax.shard_map(
        body,
        mesh=fine,
        in_specs=placed,
        out_specs=(P(AXES), P(AXES, None), P(AXES, None)),
        check_vma=False,
    )
```

```python
import jax
import jax.numpy as jnp
from jax import lax
from jax.experimental import pallas as pl
from jax.experimental.pallas import tpu as pltpu
from jax.sharding import Mesh
from jax.sharding import PartitionSpec as P

HD = 64
SQ = 32
SP = 224
S = SQ + SP
DT = 1024
DS = 768
FF = 3072
CHIPS = 64
QUARTER = 4 * HD
WIDE = 3 * DS
PAY = WIDE + 128 + DS // 2
EPS = 1e-05
LOSS_SCALE = 8.0
MIB = 1 << 20

AXES = ("zh", "zl", "y", "xh", "xl", "c")
DP = ("zl", "y", "xh", "xl", "c")
X = ("xh", "xl")
CHIP_AXES = ("zh", "zl", "y", "xh", "xl")
RIVALS = ("zh", "y", "xh")
SWAP = [(0, 1), (1, 0)]
BOTH = [(0, 3), (1, 2), (2, 1), (3, 0)]

F32 = jnp.float32
BF16 = jnp.bfloat16
NT = (((1,), (1,)), ((), ()))


def params(mib):
    return pltpu.CompilerParams(vmem_limit_bytes=mib * MIB)


def ring(step):
    return [(i, (i + step) % 4) for i in range(4)]


def mm(a, b):
    return jnp.dot(a, b, preferred_element_type=F32)


def mm_nt(a, b):
    return lax.dot_general(a, b, NT, preferred_element_type=F32)


def iota(shape, dim):
    return lax.broadcasted_iota(jnp.int32, shape, dim)


def send_axis(piece, axis):
    return [piece] + [lax.ppermute(piece, axis, ring(step)) for step in (1, 3, 2)]


def join_axis(pieces, axis, dim):
    here, piece = lax.axis_index(axis), pieces[0]
    shape = piece.shape[:dim] + (4,) + piece.shape[dim + 1 :]
    whole = jnp.zeros(shape, piece.dtype)
    for part, step in zip(pieces, (0, 1, 3, 2)):
        start = [0] * len(shape)
        start[dim] = (here - step) % 4
        whole = lax.dynamic_update_slice(whole, part, tuple(start))
    return whole


def student_kernel(
    lens, half_ref, first_ref, q_ref, p_ref, win_hbm, wout_hbm, sums_tiles, score_ref, g_ref, gp_hbm, other_hbm,
    rows, win, wout, slope, pulled_ref, sums_ref, gp, blocks, in_sems, out_sems, wout_sem, other_sems,
):
    def load(j):
        cols = pl.ds(pl.multiple_of(j * 512, 512), 512)
        return pltpu.make_async_copy(win_hbm.at[:, cols], win.at[:, cols], in_sems.at[j])

    def save(j):
        cols = pl.ds(pl.multiple_of(j * DS, DS), DS)
        return pltpu.make_async_copy(gp.at[:, :, cols], gp_hbm.at[:, :, cols], out_sems.at[j])

    def send(i, k):
        cols = pl.ds(k * DS, DS)
        return pltpu.make_async_copy(
            blocks.at[i, :, cols], other_hbm.at[i, :, cols], other_sems.at[i * 3 + k]
        )

    load_out = pltpu.make_async_copy(wout_hbm, wout, wout_sem)
    for j in range(6):
        load(j).start()
    load_out.start()
    for i in range(2):
        rows[i * S : i * S + SQ] = q_ref[first_ref[0] + i]
        rows[i * S + SQ : (i + 1) * S] = p_ref[i]
    at_row = iota((S, 1), 0) - SQ

    def pool(values):
        sums = []
        for i in range(2):
            part = values[i * S : (i + 1) * S].astype(F32)
            sums.append(jnp.sum(part[:SQ], 0, keepdims=True))
            part = jnp.where(at_row[SQ:] < lens[i], part[SQ:], 0.0)
            sums.append(jnp.sum(part, 0, keepdims=True))
        return jnp.concatenate(sums + sums, 0)


    def forward(j, carry):
        load(j).wait()
        for part in range(2):
            cols = pl.ds(pl.multiple_of(j * 512 + part * 256, 256), 256)
            pre = mm(rows[...], win[:, cols])
            bell = jnp.exp2(pre * pre * -0.7213475204444817)
            denominator = 1.0 + jnp.abs(pre) * (0.3275911 * 0.7071067811865476)
            t = pl.reciprocal(denominator, approx=True)
            t = t * (2.0 - denominator * t)
            poly = 0.5 * 1.061405429 * t - 0.5 * 1.453152027
            poly = poly * t + 0.5 * 1.421413741
            poly = poly * t - 0.5 * 0.284496736
            poly = poly * t + 0.5 * 0.254829592
            tail = poly * t * bell
            cdf = jnp.where(pre < 0.0, tail, 1.0 - tail)
            slope[:, cols] = cdf + pre * bell * 0.3989422804014327
            sums_ref[:, cols] = pool(pre * cdf)
        return carry

    lax.fori_loop(0, FF // 512, forward, 0)
    load_out.wait()
    sums = sums_ref[...]
    high = sums.astype(BF16)
    low = (sums - high.astype(F32)).astype(BF16)
    out = mm(jnp.concatenate([high, low], 0), wout[...])
    row8 = iota((8, 1), 0)
    count = jnp.where(row8 % 2 == 0, SQ, jnp.where(row8 < 2, lens[0], lens[1])).astype(F32)
    means = (pool(rows[...]) + out[:8] + out[8:]) / count
    means = means[:4]
    centred = means - jnp.mean(means, -1, keepdims=True)
    scale = lax.rsqrt(jnp.mean(centred * centred, -1, keepdims=True) + EPS)
    unit = centred * scale
    other = jnp.concatenate([unit[1:2], unit[0:1], unit[3:4], unit[2:3]], 0)
    cross = jnp.sum(unit * other, -1, keepdims=True) * DS ** (-0.5)
    back = other * DS ** (-0.5)
    back = scale * (
        back
        - jnp.mean(back, -1, keepdims=True)
        - unit * jnp.mean(back * unit, -1, keepdims=True)
    )
    grad = (back / count[:4]).astype(BF16)
    g_ref[...] = grad
    pairs = jnp.concatenate([cross[0:1], cross[2:3]], 0)
    score_ref[...] = jnp.broadcast_to(jnp.concatenate([pairs] * 4, 0), (8, 128))
    grad8 = jnp.concatenate([grad, jnp.zeros((4, DS), BF16)], 0)
    pulled_ref[...] = mm_nt(grad8, wout[...])
    def backward(j, carry):
        for part in range(3):
            cols = pl.ds(pl.multiple_of(j * DS + part * 256, 256), 256)
            pulled = pulled_ref[:, cols]
            for i in range(2):
                gate = jnp.where(at_row < lens[i], pulled[2 * i + 1 : 2 * i + 2], 0.0)
                gp[i, SQ:, cols] = (gate[SQ:] * slope[i * S + SQ : (i + 1) * S, cols]).astype(BF16)
                gp[i, :SQ, cols] = (
                    pulled[2 * i : 2 * i + 1] * slope[i * S : i * S + SQ, cols]
                ).astype(BF16)
        save(j).start()
        return carry

    lax.fori_loop(0, FF // DS, backward, 0)
    fill = jnp.zeros((4, 16), F32)
    for d in range(CHIPS):
        part = sums[:4, d * 48 : d * 48 + 48]
        sums_tiles[d] = jnp.concatenate([part, fill, part, fill], 1)
    grad_blocks(
        half_ref[0], rows, gp, blocks, lambda i, k: send(i, k).start()
    )
    for j in range(FF // DS):
        save(j).wait()
    for j in range(6):
        send(j // 3, j % 3).wait()


def student(lens, half, first, queries, passages, w_in, w_out):
    vmem = pl.BlockSpec(memory_space=pltpu.VMEM)
    anywhere = pl.BlockSpec(memory_space=pl.ANY)
    return pl.pallas_call(
        student_kernel,
        out_shape=(
            jax.ShapeDtypeStruct((CHIPS, 4, 128), F32),
            jax.ShapeDtypeStruct((8, 128), F32),
            jax.ShapeDtypeStruct((4, DS), BF16),
            jax.ShapeDtypeStruct((2, S, FF), BF16),
            jax.ShapeDtypeStruct((2, 8 * CHIPS, WIDE), BF16),
        ),
        in_specs=[pl.BlockSpec(memory_space=pltpu.SMEM)] * 3 + [vmem, vmem, anywhere, anywhere],
        out_specs=(vmem, vmem, vmem, anywhere, anywhere),
        scratch_shapes=[
            pltpu.VMEM((2 * S, DS), BF16),
            pltpu.VMEM((DS, FF), BF16),
            pltpu.VMEM((FF, DS), BF16),
            pltpu.VMEM((2 * S, FF), F32),
            pltpu.VMEM((8, FF), F32),
            pltpu.VMEM((8, FF), F32),
            pltpu.VMEM((2, S, FF), BF16),
            pltpu.VMEM((2, 8 * CHIPS, WIDE), BF16),
            pltpu.SemaphoreType.DMA((6,)),
            pltpu.SemaphoreType.DMA((4,)),
            pltpu.SemaphoreType.DMA,
            pltpu.SemaphoreType.DMA((6,)),
        ],
        compiler_params=params(60),
        cost_estimate=pl.CostEstimate(flops=1, bytes_accessed=1, transcendentals=0),
        name="student",
    )(lens, half.reshape(1), first.reshape(1), queries, passages, w_in, w_out)


def select_features(half, rows):
    line, feature = iota((8 * CHIPS, DS), 0), iota((8 * CHIPS, DS), 1)
    lane = line % 8
    wanted = jnp.where(lane < 6, (2 * (line // 8) + half) * 6 + lane, -1)
    return mm_nt(jnp.where(feature == wanted, 1.0, 0.0).astype(BF16), rows)


def late_features(wide, k):
    lane = iota((8 * CHIPS, S), 0) % 8
    return jnp.where(
        lane == 6,
        pltpu.roll(wide, 6 - k, 0),
        jnp.where(lane == 7, pltpu.roll(wide, 4 - k, 0), 0.0),
    ).astype(BF16)


def grad_blocks(half, rows, grad, out, done):
    for i in range(2):
        wide = select_features(half, rows[i * S : (i + 1) * S])
        main = wide.astype(BF16)
        for k in range(3):
            rest = late_features(wide, k)
            for part in range(3):
                at = k * DS + part * 256
                late = 3 * DS + part * 256
                out[i, :, at : at + 256] = (
                    mm(main, grad[i, :, at : at + 256]) + mm(rest, grad[i, :, late : late + 256])
                ).astype(BF16)
            done(i, k)


def first_kernel(half_ref, first_ref, q_ref, p_ref, gp_hbm, out_hbm, gp, out, gp_sems, out_sems):
    def block(ref, k):
        return ref.at[:, pl.ds(k * DS, DS)]

    def load(k):
        return pltpu.make_async_copy(block(gp_hbm.at[0], k), block(gp, k), gp_sems.at[k])

    def save(k):
        return pltpu.make_async_copy(block(out, k), block(out_hbm, k), out_sems.at[k])

    for k in (3, 0, 1, 2):
        load(k).start()
    wide = select_features(half_ref[0], jnp.concatenate([q_ref[first_ref[0]], p_ref[0]], 0))
    main = wide.astype(BF16)
    load(3).wait()
    for k in range(3):
        rest = late_features(wide, k)
        load(k).wait()
        for part in range(3):
            cols = slice(k * DS + part * 256, k * DS + part * 256 + 256)
            late = slice(3 * DS + part * 256, 3 * DS + part * 256 + 256)
            out[:, cols] = (mm(main, gp[:, cols]) + mm(rest, gp[:, late])).astype(BF16)
        save(k).start()
    for k in range(3):
        save(k).wait()


def first_term(half, first, queries, passages, grad_pre):
    vmem = pl.BlockSpec(memory_space=pltpu.VMEM)
    anywhere = pl.BlockSpec(memory_space=pl.ANY)
    return pl.pallas_call(
        first_kernel,
        out_shape=jax.ShapeDtypeStruct((8 * CHIPS, WIDE), BF16),
        in_specs=[pl.BlockSpec(memory_space=pltpu.SMEM)] * 2 + [vmem, vmem, anywhere],
        out_specs=anywhere,
        scratch_shapes=[
            pltpu.VMEM((S, FF), BF16),
            pltpu.VMEM((8 * CHIPS, WIDE), BF16),
            pltpu.SemaphoreType.DMA((4,)),
            pltpu.SemaphoreType.DMA((3,)),
        ],
        compiler_params=params(60),
        cost_estimate=pl.CostEstimate(flops=3 * 10**9, bytes_accessed=4 * 10**6, transcendentals=0),
        name="first_term",
    )(half.reshape(1), first.reshape(1), queries, passages, grad_pre)


def turn(values, shift):
    wide = values.shape[1] // 2
    amount = shift * 128
    return jnp.concatenate(
        [pltpu.roll(values[:, :wide], amount, 1), pltpu.roll(values[:, wide:], amount, 1)], 1
    )


def teacher_kernel(
    y_ref, x0, x1, x2, x3, w0, w1, w2, w3, student_ref, near_ref, flip_ref, far_ref, farflip_ref,
    hidden, weight, starts, x_sems, w_sems, sems,
):
    copies, heads = [], []
    for i, ref in enumerate((w0, w1, w2, w3)):
        copies.append(pltpu.make_async_copy(ref, weight.at[i], w_sems.at[i]))
    for i, ref in enumerate((x0, x1, x2, x3)):
        for j in range(2):
            heads.append(
                pltpu.make_async_copy(ref.at[pl.ds(j * S, 16)], starts.at[i, j], sems.at[i, j])
            )
        copies.append(pltpu.make_async_copy(ref, hidden.at[i], x_sems.at[i]))
    for copy in heads + copies:
        copy.start()
    xs, ws = [hidden.at[i] for i in range(4)], [weight.at[i] for i in range(4)]
    there, back = (4 - y_ref[0]) % 4, y_ref[0]
    blocks = [(ws[m], z, (z * 4 + m) * 128) for z in range(2) for m in range(4)]

    def reduce(values, first):
        total = None
        for ref, z, at in blocks:
            term = mm(values[:, at : at + 128], ref[z, :, first : first + QUARTER])
            total = term if total is None else total + term
        return total

    def expand(values, first):
        return jnp.concatenate(
            [mm_nt(values, ref[z, :, first : first + QUARTER]) for ref, z, _ in blocks], 1
        )

    for copy in heads + copies[:4]:
        copy.wait()
    lead = jnp.concatenate([starts[i, j, :1] for i in range(4) for j in range(2)], 0).astype(F32)
    query = reduce(turn(lead, there).astype(BF16), 0).astype(BF16).astype(F32)
    head, col = iota((32, QUARTER), 0) // 8, iota((32, QUARTER), 1) // HD
    spread = jnp.where(head == col, jnp.concatenate([query] * 4, 0), 0.0).astype(BF16)
    keyed = turn(expand(spread, QUARTER), back).astype(BF16)
    logits = []
    for copy, x in zip(copies[4:], xs):
        copy.wait()
        logits.append(mm_nt(keyed, x[: 2 * S]))
    logits = jnp.concatenate(logits, 1) * HD ** (-0.5)
    live = jnp.concatenate([x[2 * S : 2 * S + 1, : 2 * S].astype(F32) for x in xs], 1)
    pair, slot = iota((32, 8 * S), 0) % 8, iota((32, 8 * S), 1) // S
    logits = jnp.where((pair == slot) & (live > 0.5), logits, -1e30)
    weights = jnp.exp(logits - jnp.max(logits, -1, keepdims=True))
    weights = (weights / jnp.sum(weights, -1, keepdims=True)).astype(BF16)
    mixed = mm(weights[:, : 2 * S], xs[0][: 2 * S])
    for i in range(1, 4):
        mixed += mm(weights[:, i * 2 * S : (i + 1) * 2 * S], xs[i][: 2 * S])
    context = reduce(turn(mixed, there).astype(BF16), 2 * QUARTER)
    context = jnp.where(head == col, context, 0.0)
    context = (context[:8] + context[8:16] + context[16:24] + context[24:]).astype(BF16)
    projected = turn(expand(context, 3 * QUARTER), back)
    own = projected[:2] + lead[:2]
    core, far, both = projected[2:4], projected[4:6], projected[6:]
    for ref, order in (
        (near_ref, (own, core, far, both)),
        (flip_ref, (core, own, both, far)),
        (far_ref, (far, both, own, core)),
        (farflip_ref, (both, far, core, own)),
    ):
        ref[:, :DT] = jnp.concatenate(order, 0)
        ref[:, DT:] = student_ref[...]


def teacher_partial(y, xs, ws, student_scores):
    shape = jax.ShapeDtypeStruct((8, DT + 128), F32)
    vmem = pl.BlockSpec(memory_space=pltpu.VMEM)
    return pl.pallas_call(
        teacher_kernel,
        out_shape=(shape,) * 4,
        in_specs=[pl.BlockSpec(memory_space=pltpu.SMEM)]
        + [pl.BlockSpec(memory_space=pl.ANY)] * 8
        + [vmem],
        out_specs=(vmem,) * 4,
        scratch_shapes=[
            pltpu.VMEM((4, 2 * S + 16, DT), BF16),
            pltpu.VMEM((4, 2, 128, DT), BF16),
            pltpu.VMEM((4, 2, 16, DT), BF16),
            pltpu.SemaphoreType.DMA((4,)),
            pltpu.SemaphoreType.DMA((4,)),
            pltpu.SemaphoreType.DMA((4, 2)),
        ],
        compiler_params=params(24),
        cost_estimate=pl.CostEstimate(flops=10**9, bytes_accessed=6 * 10**6, transcendentals=0),
        name="teacher_partial",
    )(y.reshape(1), *xs, *ws, student_scores)


def score_kernel(own, core, far, both, gain, weight, tile_ref, spread_ref, score_ref):
    refs = (own, core, far, both)
    values = own[:, :DT] + core[:, :DT] + far[:, :DT] + both[:, :DT]
    centred = values - jnp.mean(values, -1, keepdims=True)
    unit = centred * lax.rsqrt(jnp.mean(centred * centred, -1, keepdims=True) + EPS)
    score = jnp.sum(unit * gain[...] * weight[...], -1, keepdims=True)
    student = jnp.concatenate([ref[:2, DT:] for ref in refs], 0)
    tile = jnp.where(iota((8, 128), 1) < 64, score, student)
    tile_ref[...] = tile
    for i in range(2):
        score_ref[i] = jnp.sum(score[i : i + 1])
    for i in range(16):
        spread_ref[i] = tile


def score_tile(parts, gain, weight):
    vmem = pl.BlockSpec(memory_space=pltpu.VMEM)
    return pl.pallas_call(
        score_kernel,
        out_shape=(
            jax.ShapeDtypeStruct((8, 128), F32),
            jax.ShapeDtypeStruct((16, 8, 128), F32),
            jax.ShapeDtypeStruct((2,), F32),
        ),
        in_specs=[vmem] * 6,
        out_specs=(vmem, vmem, pl.BlockSpec(memory_space=pltpu.SMEM)),
        compiler_params=params(8),
        name="score_tile",
    )(*parts, gain, weight)


def payload_kernel(
    half_ref, first_ref, tile_ref, all_ref, q_ref, p_ref, gp_hbm, first_hbm, recv_hbm, sums_ref, g_ref, out_hbm,
    gp, term, recv, out, gp_sems, term_sems, recv_sems, out_sems,
):
    def load_grad(k):
        cols = pl.ds(k * DS, DS)
        return pltpu.make_async_copy(gp_hbm.at[1, :, cols], gp.at[:, cols], gp_sems.at[k])

    def load_first(k):
        cols = pl.ds(k * DS, DS)
        return pltpu.make_async_copy(first_hbm.at[:, cols], term.at[:, cols], term_sems.at[k])

    def load_term(k):
        cols = pl.ds(k * DS, DS)
        return pltpu.make_async_copy(recv_hbm.at[:, :, cols], recv.at[:, :, cols], recv_sems.at[k])

    def save(k):
        cols = pl.ds(k * DS, DS) if k < 3 else pl.ds(WIDE, PAY - WIDE)
        return pltpu.make_async_copy(out.at[:, cols], out_hbm.at[:, cols], out_sems.at[k])

    load_grad(3).start()
    for k in range(3):
        load_grad(k).start()
        load_first(k).start()
        load_term(k).start()
    every = jnp.concatenate([all_ref[:, :4], all_ref[:, 4:]], 0)
    top = jnp.max(every, 0)
    lse = top + jnp.log(jnp.sum(jnp.exp(every - top[None]), 0))
    share = jnp.exp(tile_ref[:4] - lse)
    cot = LOSS_SCALE * (share[:, 64:65] - share[:, :1])
    rows = jnp.concatenate([q_ref[first_ref[0] + 1], p_ref[1]], 0)
    wide = select_features(half_ref[0], rows) * cot[1:2]
    main = wide.astype(BF16)
    by_group = jnp.concatenate([cot[j : j + 1] for j in range(2) for _ in range(2)], 0)
    scaled = sums_ref[...] * by_group[None]
    high = scaled.astype(BF16).astype(F32)
    scaled = jnp.where(iota((CHIPS, 4, 128), 2) < 64, high, scaled - high)
    scaled = jnp.concatenate([scaled, scaled], 1).reshape(8 * CHIPS, 128)
    out[:, WIDE : WIDE + 128] = scaled.astype(BF16)
    grad = g_ref[...].astype(F32)
    grad = jnp.concatenate([grad[:, : DS // 2], grad[:, DS // 2 :]], 0)
    out[:, WIDE + 128 :] = jnp.concatenate([grad] * CHIPS, 0).astype(BF16)
    save(3).start()
    load_grad(3).wait()
    for k in range(3):
        rest = late_features(wide, k)
        load_grad(k).wait()
        load_first(k).wait()
        load_term(k).wait()
        for part in range(3):
            cols = slice(k * DS + part * 256, k * DS + part * 256 + 256)
            late = slice(3 * DS + part * 256, 3 * DS + part * 256 + 256)
            total = mm(main, gp[:, cols]) + mm(rest, gp[:, late])
            total += term[:, cols].astype(F32) * cot[:1]
            for i in range(2):
                total += recv[i, :, cols].astype(F32) * cot[2 + i : 3 + i]
            out[:, cols] = total.astype(BF16)
        save(k).start()
    for k in range(4):
        save(k).wait()


def payload(half, first, tile, every, queries, passages, grad_pre, term, received, sums, grad):
    vmem = pl.BlockSpec(memory_space=pltpu.VMEM)
    anywhere = pl.BlockSpec(memory_space=pl.ANY)
    return pl.pallas_call(
        payload_kernel,
        out_shape=jax.ShapeDtypeStruct((CHIPS * 8, PAY), BF16),
        in_specs=[pl.BlockSpec(memory_space=pltpu.SMEM)] * 2
        + [vmem] * 4
        + [anywhere, anywhere, anywhere, vmem, vmem],
        out_specs=anywhere,
        scratch_shapes=[
            pltpu.VMEM((S, FF), BF16),
            pltpu.VMEM((8 * CHIPS, WIDE), BF16),
            pltpu.VMEM((2, 8 * CHIPS, WIDE), BF16),
            pltpu.VMEM((8 * CHIPS, PAY), BF16),
            pltpu.SemaphoreType.DMA((4,)),
            pltpu.SemaphoreType.DMA((3,)),
            pltpu.SemaphoreType.DMA((3,)),
            pltpu.SemaphoreType.DMA((4,)),
        ],
        compiler_params=params(60),
        name="payload",
    )(
        half.reshape(1), first.reshape(1), tile, every, queries, passages, grad_pre, term, received,
        sums, grad,
    )


def sum_kernel(in_ref, gin_ref):
    total = in_ref[0, :, :WIDE].astype(F32)
    for d in range(1, CHIPS):
        total += in_ref[d, :, :WIDE].astype(F32)
    gin_ref[:, :WIDE] = total[:6]
    for r in range(6):
        line, at = 6 + r // 3, r % 3 * DS
        gin_ref[r : r + 1, WIDE:] = total[line : line + 1, at : at + DS]


def sum_terms(incoming):
    vmem = pl.BlockSpec(memory_space=pltpu.VMEM)
    return pl.pallas_call(
        sum_kernel,
        out_shape=jax.ShapeDtypeStruct((6, FF), F32),
        in_specs=[vmem],
        out_specs=vmem,
        compiler_params=params(32),
        name="sum_terms",
    )(incoming)


def outer_kernel(core_ref, in_ref, own_ref, send_ref):
    columns = in_ref[:, :, WIDE : WIDE + 128].astype(F32).reshape(CHIPS * 8, 128).T
    line = iota((128, CHIPS * 8), 1) % 8
    grads = in_ref[:, :, WIDE + 128 :].astype(F32).reshape(CHIPS * 8, DS // 2).astype(BF16)
    left = mm(jnp.where(line < 4, columns, 0.0).astype(BF16), grads)
    right = mm(jnp.where(line < 4, 0.0, columns).astype(BF16), grads)
    both = jnp.concatenate([left[:48] + left[64:112], right[:48] + right[64:112]], 1)
    first = core_ref[0] == 0
    own_ref[...] = jnp.where(first, both[:24], both[24:])
    send_ref[...] = jnp.where(first, both[24:], both[:24])


def outer_terms(core, incoming):
    vmem = pl.BlockSpec(memory_space=pltpu.VMEM)
    part = jax.ShapeDtypeStruct((24, DS), F32)
    return pl.pallas_call(
        outer_kernel,
        out_shape=(part, part),
        in_specs=[pl.BlockSpec(memory_space=pltpu.SMEM), vmem],
        out_specs=(vmem,) * 2,
        compiler_params=params(32),
        name="outer_terms",
    )(core.reshape(1), incoming)


def pack_kernel(me_ref, qkv_ref, out_ref, p0, p1, p2, p3):
    for flip, ref in enumerate((p0, p1, p2, p3)):
        for j in range(4):

            @pl.when(me_ref[0] == j)
            def _():
                who = j ^ flip
                for t in range(3):
                    at = t * DT + who * QUARTER
                    ref[0, :, t * QUARTER : (t + 1) * QUARTER] = qkv_ref[:, at : at + QUARTER]
                ref[0, :, 3 * QUARTER :] = out_ref[:, who * QUARTER : (who + 1) * QUARTER]


def pack_weights(me, qkv_weight, out_weight):
    vmem = pl.BlockSpec(memory_space=pltpu.VMEM)
    return pl.pallas_call(
        pack_kernel,
        out_shape=(jax.ShapeDtypeStruct((1, 16, DT), BF16),) * 4,
        in_specs=[pl.BlockSpec(memory_space=pltpu.SMEM), vmem, vmem],
        out_specs=(vmem,) * 4,
        compiler_params=params(8),
        name="pack_weights",
    )(me.reshape(1), qkv_weight, out_weight.T)


def exchange_weights(qkv_weight, out_weight):
    me = 2 * lax.axis_index("zl") + lax.axis_index("c")
    mine, to_core, to_far, to_both = pack_weights(me, qkv_weight, out_weight)
    from_core = lax.ppermute(to_core, "c", SWAP)
    from_far = lax.ppermute(to_far, "zl", SWAP)
    from_both = lax.ppermute(to_both, ("zl", "c"), BOTH)
    four = jnp.zeros((4, 16, DT), BF16)
    for part, who in ((mine, me), (from_core, me ^ 1), (from_far, me ^ 2), (from_both, me ^ 3)):
        four = lax.dynamic_update_slice(four, part, (who, 0, 0))
    return four.reshape(2, 1, 1, 32, DT)


def body(
    teacher_hidden,
    passage_len,
    qkv_weight,
    out_weight,
    teacher_gain,
    score_weight,
    query_tokens,
    passage_tokens,
    w_in,
    w_out,
):
    core = lax.axis_index("c")
    first = lax.axis_index("xl") * 4 + core * 2

    slots = jnp.arange(S)
    live = (slots[None, :] < SQ) | (slots[None, :] - SQ < passage_len[:, None])
    live = jnp.pad(live.astype(BF16).reshape(1, 2 * S), ((0, 15), (0, DT - 2 * S)))
    hidden = jnp.concatenate([teacher_hidden.reshape(2 * S, DT), live], 0)

    four = exchange_weights(qkv_weight, out_weight)
    four, hidden = lax.optimization_barrier((four, hidden))
    hidden_far = lax.ppermute(hidden, "zl", SWAP)
    hidden_core = lax.ppermute(hidden, "c", SWAP)
    plane = join_axis(send_axis(four, X), X, 2)
    plane, early_query, hidden_core = lax.optimization_barrier((plane, query_tokens, hidden_core))
    planes = send_axis(plane, "y")

    sums, student_scores, grad, grad_pre, other = student(
        passage_len, 1 - core, first, early_query, passage_tokens, w_in, w_out
    )

    planes, other, hidden_far = lax.optimization_barrier((planes, other, hidden_far))
    hidden_both = lax.ppermute(hidden_far, "c", SWAP)
    here, before, after, across = [part.reshape(2, 128, DT) for part in planes]
    near, flip, far, farflip = teacher_partial(
        lax.axis_index("y"),
        (hidden, hidden_core, hidden_far, hidden_both),
        (here, after, across, before),
        student_scores,
    )
    parts = (
        near,
        lax.ppermute(flip, "c", SWAP),
        lax.ppermute(far, "zl", SWAP),
        lax.ppermute(farflip, ("zl", "c"), BOTH),
    )
    tile, spread, scores = score_tile(parts, teacher_gain[None], score_weight[None])
    every = lax.all_to_all(spread, RIVALS, 0, 0, tiled=True)
    other, late_query, _ = lax.optimization_barrier((other, query_tokens, tile))
    received = lax.ppermute(other, "c", SWAP)
    term = first_term(core, first, late_query, passage_tokens, grad_pre)
    outgoing = payload(
        core, first, tile, every, query_tokens, passage_tokens, grad_pre, term, received, sums, grad
    )
    incoming = lax.all_to_all(outgoing.reshape(CHIPS, 8, PAY), CHIP_AXES, 0, 0, tiled=True)
    own_out, send_out = outer_terms(core, incoming)
    grad_in = sum_terms(incoming)
    return (scores, grad_in, own_out + lax.ppermute(send_out, "c", SWAP))


def solution(mesh):
    fine = Mesh(mesh.devices.reshape(2, 2, 4, 2, 2, 2), AXES)
    placed = (
        P(AXES, None, None),
        P(AXES),
        P(DP, None),
        P(None, DP),
        P(),
        P(),
        P(),
        P(AXES, None, None),
        P(),
        P(),
    )
    return jax.shard_map(
        body,
        mesh=fine,
        in_specs=placed,
        out_specs=(P(AXES), P(AXES, None), P(AXES, None)),
        check_vma=False,
    )
```

```python
import jax
import jax.numpy as jnp
from jax import lax
from jax.experimental import pallas as pl
from jax.experimental.pallas import tpu as pltpu
from jax.sharding import Mesh
from jax.sharding import PartitionSpec as P

HD = 64
SQ = 32
SP = 224
S = SQ + SP
DT = 1024
DS = 768
FF = 3072
CHIPS = 64
QUARTER = 4 * HD
WIDE = 3 * DS
PAY = WIDE + 128 + DS // 2
EPS = 1e-05
LOSS_SCALE = 8.0
MIB = 1 << 20

AXES = ("zh", "zl", "y", "xh", "xl", "c")
DP = ("zl", "y", "xh", "xl", "c")
X = ("xh", "xl")
CHIP_AXES = ("zh", "zl", "y", "xh", "xl")
RIVALS = ("zh", "y", "xh")
SWAP = [(0, 1), (1, 0)]
BOTH = [(0, 3), (1, 2), (2, 1), (3, 0)]

F32 = jnp.float32
BF16 = jnp.bfloat16
NT = (((1,), (1,)), ((), ()))


def params(mib):
    return pltpu.CompilerParams(vmem_limit_bytes=mib * MIB)


def ring(step):
    return [(i, (i + step) % 4) for i in range(4)]


def mm(a, b):
    return jnp.dot(a, b, preferred_element_type=F32)


def mm_nt(a, b):
    return lax.dot_general(a, b, NT, preferred_element_type=F32)


def iota(shape, dim):
    return lax.broadcasted_iota(jnp.int32, shape, dim)


def send_axis(piece, axis):
    return [piece] + [lax.ppermute(piece, axis, ring(step)) for step in (1, 3, 2)]


def join_axis(pieces, axis, dim):
    here, piece = lax.axis_index(axis), pieces[0]
    shape = piece.shape[:dim] + (4,) + piece.shape[dim + 1 :]
    whole = jnp.zeros(shape, piece.dtype)
    for part, step in zip(pieces, (0, 1, 3, 2)):
        start = [0] * len(shape)
        start[dim] = (here - step) % 4
        whole = lax.dynamic_update_slice(whole, part, tuple(start))
    return whole


def student_kernel(
    lens, half_ref, first_ref, q_ref, p_ref, win_hbm, wout_hbm, sums_tiles, score_ref, g_ref, gp_hbm, other_hbm,
    rows, win, wout, slope, pulled_ref, sums_ref, gp, blocks, in_sems, out_sems, wout_sem, other_sems,
):
    def load(j):
        cols = pl.ds(pl.multiple_of(j * 512, 512), 512)
        return pltpu.make_async_copy(win_hbm.at[:, cols], win.at[:, cols], in_sems.at[j])

    def save(j):
        cols = pl.ds(pl.multiple_of(j * DS, DS), DS)
        return pltpu.make_async_copy(gp.at[:, :, cols], gp_hbm.at[:, :, cols], out_sems.at[j])

    def send(i, k):
        cols = pl.ds(k * DS, DS)
        return pltpu.make_async_copy(
            blocks.at[i, :, cols], other_hbm.at[i, :, cols], other_sems.at[i * 3 + k]
        )

    load_out = pltpu.make_async_copy(wout_hbm, wout, wout_sem)
    for j in range(6):
        load(j).start()
    load_out.start()
    for i in range(2):
        rows[i * S : i * S + SQ] = q_ref[first_ref[0] + i]
        rows[i * S + SQ : (i + 1) * S] = p_ref[i]
    at_row = iota((S, 1), 0) - SQ

    def pool(values):
        sums = []
        for i in range(2):
            part = values[i * S : (i + 1) * S].astype(F32)
            sums.append(jnp.sum(part[:SQ], 0, keepdims=True))
            part = jnp.where(at_row[SQ:] < lens[i], part[SQ:], 0.0)
            sums.append(jnp.sum(part, 0, keepdims=True))
        return jnp.concatenate(sums + sums, 0)


    def forward(j, carry):
        load(j).wait()
        for part in range(2):
            cols = pl.ds(pl.multiple_of(j * 512 + part * 256, 256), 256)
            pre = mm(rows[...], win[:, cols])
            bell = jnp.exp2(pre * pre * -0.7213475204444817)
            denominator = 1.0 + jnp.abs(pre) * (0.3275911 * 0.7071067811865476)
            t = pl.reciprocal(denominator, approx=True)
            t = t * (2.0 - denominator * t)
            poly = 0.5 * 1.061405429 * t - 0.5 * 1.453152027
            poly = poly * t + 0.5 * 1.421413741
            poly = poly * t - 0.5 * 0.284496736
            poly = poly * t + 0.5 * 0.254829592
            tail = poly * t * bell
            cdf = jnp.where(pre < 0.0, tail, 1.0 - tail)
            slope[:, cols] = cdf + pre * bell * 0.3989422804014327
            sums_ref[:, cols] = pool(pre * cdf)
        return carry

    lax.fori_loop(0, FF // 512, forward, 0)
    load_out.wait()
    sums = sums_ref[...]
    high = sums.astype(BF16)
    low = (sums - high.astype(F32)).astype(BF16)
    out = mm(jnp.concatenate([high, low], 0), wout[...])
    row8 = iota((8, 1), 0)
    count = jnp.where(row8 % 2 == 0, SQ, jnp.where(row8 < 2, lens[0], lens[1])).astype(F32)
    means = (pool(rows[...]) + out[:8] + out[8:]) / count
    means = means[:4]
    centred = means - jnp.mean(means, -1, keepdims=True)
    scale = lax.rsqrt(jnp.mean(centred * centred, -1, keepdims=True) + EPS)
    unit = centred * scale
    other = jnp.concatenate([unit[1:2], unit[0:1], unit[3:4], unit[2:3]], 0)
    cross = jnp.sum(unit * other, -1, keepdims=True) * DS ** (-0.5)
    back = other * DS ** (-0.5)
    back = scale * (
        back
        - jnp.mean(back, -1, keepdims=True)
        - unit * jnp.mean(back * unit, -1, keepdims=True)
    )
    grad = (back / count[:4]).astype(BF16)
    g_ref[...] = grad
    pairs = jnp.concatenate([cross[0:1], cross[2:3]], 0)
    score_ref[...] = jnp.broadcast_to(jnp.concatenate([pairs] * 4, 0), (8, 128))
    grad8 = jnp.concatenate([grad, jnp.zeros((4, DS), BF16)], 0)
    pulled_ref[...] = mm_nt(grad8, wout[...])
    def backward(j):
        for part in range(3):
            cols = slice(j * DS + part * 256, j * DS + part * 256 + 256)
            pulled = pulled_ref[:, cols]
            for i in range(2):
                gate = jnp.where(at_row < lens[i], pulled[2 * i + 1 : 2 * i + 2], 0.0)
                gp[i, SQ:, cols] = (gate[SQ:] * slope[i * S + SQ : (i + 1) * S, cols]).astype(BF16)
                gp[i, :SQ, cols] = (
                    pulled[2 * i : 2 * i + 1] * slope[i * S : i * S + SQ, cols]
                ).astype(BF16)
        save(j).start()

    backward(3)
    backward(0)
    fill = jnp.zeros((4, 16), F32)
    for d in range(CHIPS):
        part = sums[:4, d * 48 : d * 48 + 48]
        sums_tiles[d] = jnp.concatenate([part, fill, part, fill], 1)
    grad_blocks(
        half_ref[0],
        rows,
        gp,
        blocks,
        ahead=lambda k: backward(k + 1) if k < 2 else None,
        done=lambda i, k: send(i, k).start(),
    )
    for j in range(FF // DS):
        save(j).wait()
    for j in range(6):
        send(j // 3, j % 3).wait()


def student(lens, half, first, queries, passages, w_in, w_out):
    vmem = pl.BlockSpec(memory_space=pltpu.VMEM)
    anywhere = pl.BlockSpec(memory_space=pl.ANY)
    return pl.pallas_call(
        student_kernel,
        out_shape=(
            jax.ShapeDtypeStruct((CHIPS, 4, 128), F32),
            jax.ShapeDtypeStruct((8, 128), F32),
            jax.ShapeDtypeStruct((4, DS), BF16),
            jax.ShapeDtypeStruct((2, S, FF), BF16),
            jax.ShapeDtypeStruct((2, 8 * CHIPS, WIDE), BF16),
        ),
        in_specs=[pl.BlockSpec(memory_space=pltpu.SMEM)] * 3 + [vmem, vmem, anywhere, anywhere],
        out_specs=(vmem, vmem, vmem, anywhere, anywhere),
        scratch_shapes=[
            pltpu.VMEM((2 * S, DS), BF16),
            pltpu.VMEM((DS, FF), BF16),
            pltpu.VMEM((FF, DS), BF16),
            pltpu.VMEM((2 * S, FF), F32),
            pltpu.VMEM((8, FF), F32),
            pltpu.VMEM((8, FF), F32),
            pltpu.VMEM((2, S, FF), BF16),
            pltpu.VMEM((2, 8 * CHIPS, WIDE), BF16),
            pltpu.SemaphoreType.DMA((6,)),
            pltpu.SemaphoreType.DMA((4,)),
            pltpu.SemaphoreType.DMA,
            pltpu.SemaphoreType.DMA((6,)),
        ],
        compiler_params=params(60),
        cost_estimate=pl.CostEstimate(flops=1, bytes_accessed=1, transcendentals=0),
        name="student",
    )(lens, half.reshape(1), first.reshape(1), queries, passages, w_in, w_out)


def select_features(half, rows):
    line, feature = iota((8 * CHIPS, DS), 0), iota((8 * CHIPS, DS), 1)
    lane = line % 8
    wanted = jnp.where(lane < 6, (2 * (line // 8) + half) * 6 + lane, -1)
    return mm_nt(jnp.where(feature == wanted, 1.0, 0.0).astype(BF16), rows)


def late_features(wide, k):
    lane = iota((8 * CHIPS, S), 0) % 8
    return jnp.where(
        lane == 6,
        pltpu.roll(wide, 6 - k, 0),
        jnp.where(lane == 7, pltpu.roll(wide, 4 - k, 0), 0.0),
    ).astype(BF16)


def grad_blocks(half, rows, grad, out, ahead, done):
    wide = [select_features(half, rows[i * S : (i + 1) * S]) for i in range(2)]
    main = [values.astype(BF16) for values in wide]
    for k in range(3):
        ahead(k)
        for i in range(2):
            rest = late_features(wide[i], k)
            for part in range(3):
                at = k * DS + part * 256
                late = 3 * DS + part * 256
                out[i, :, at : at + 256] = (
                    mm(main[i], grad[i, :, at : at + 256]) + mm(rest, grad[i, :, late : late + 256])
                ).astype(BF16)
            done(i, k)


def first_kernel(half_ref, first_ref, q_ref, p_ref, gp_hbm, out_hbm, gp, out, gp_sems, out_sems):
    def block(ref, k):
        return ref.at[:, pl.ds(k * DS, DS)]

    def load(k):
        return pltpu.make_async_copy(block(gp_hbm.at[0], k), block(gp, k), gp_sems.at[k])

    def save(k):
        return pltpu.make_async_copy(block(out, k), block(out_hbm, k), out_sems.at[k])

    for k in (3, 0, 1, 2):
        load(k).start()
    wide = select_features(half_ref[0], jnp.concatenate([q_ref[first_ref[0]], p_ref[0]], 0))
    main = wide.astype(BF16)
    load(3).wait()
    for k in range(3):
        rest = late_features(wide, k)
        load(k).wait()
        for part in range(3):
            cols = slice(k * DS + part * 256, k * DS + part * 256 + 256)
            late = slice(3 * DS + part * 256, 3 * DS + part * 256 + 256)
            out[:, cols] = (mm(main, gp[:, cols]) + mm(rest, gp[:, late])).astype(BF16)
        save(k).start()
    for k in range(3):
        save(k).wait()


def first_term(half, first, queries, passages, grad_pre):
    vmem = pl.BlockSpec(memory_space=pltpu.VMEM)
    anywhere = pl.BlockSpec(memory_space=pl.ANY)
    return pl.pallas_call(
        first_kernel,
        out_shape=jax.ShapeDtypeStruct((8 * CHIPS, WIDE), BF16),
        in_specs=[pl.BlockSpec(memory_space=pltpu.SMEM)] * 2 + [vmem, vmem, anywhere],
        out_specs=anywhere,
        scratch_shapes=[
            pltpu.VMEM((S, FF), BF16),
            pltpu.VMEM((8 * CHIPS, WIDE), BF16),
            pltpu.SemaphoreType.DMA((4,)),
            pltpu.SemaphoreType.DMA((3,)),
        ],
        compiler_params=params(60),
        cost_estimate=pl.CostEstimate(flops=3 * 10**9, bytes_accessed=4 * 10**6, transcendentals=0),
        name="first_term",
    )(half.reshape(1), first.reshape(1), queries, passages, grad_pre)


def turn(values, shift):
    wide = values.shape[1] // 2
    amount = shift * 128
    return jnp.concatenate(
        [pltpu.roll(values[:, :wide], amount, 1), pltpu.roll(values[:, wide:], amount, 1)], 1
    )


def teacher_kernel(
    y_ref, x0, x1, x2, x3, w0, w1, w2, w3, student_ref, near_ref, flip_ref, far_ref, farflip_ref,
    hidden, weight, starts, x_sems, w_sems, sems,
):
    copies, heads = [], []
    for i, ref in enumerate((w0, w1, w2, w3)):
        copies.append(pltpu.make_async_copy(ref, weight.at[i], w_sems.at[i]))
    for i, ref in enumerate((x0, x1, x2, x3)):
        for j in range(2):
            heads.append(
                pltpu.make_async_copy(ref.at[pl.ds(j * S, 16)], starts.at[i, j], sems.at[i, j])
            )
        copies.append(pltpu.make_async_copy(ref, hidden.at[i], x_sems.at[i]))
    for copy in heads + copies:
        copy.start()
    xs, ws = [hidden.at[i] for i in range(4)], [weight.at[i] for i in range(4)]
    there, back = (4 - y_ref[0]) % 4, y_ref[0]
    blocks = [(ws[m], z, (z * 4 + m) * 128) for z in range(2) for m in range(4)]

    def reduce(values, first):
        total = None
        for ref, z, at in blocks:
            term = mm(values[:, at : at + 128], ref[z, :, first : first + QUARTER])
            total = term if total is None else total + term
        return total

    def expand(values, first):
        return jnp.concatenate(
            [mm_nt(values, ref[z, :, first : first + QUARTER]) for ref, z, _ in blocks], 1
        )

    for copy in heads + copies[:4]:
        copy.wait()
    lead = jnp.concatenate([starts[i, j, :1] for i in range(4) for j in range(2)], 0).astype(F32)
    query = reduce(turn(lead, there).astype(BF16), 0).astype(BF16).astype(F32)
    head, col = iota((32, QUARTER), 0) // 8, iota((32, QUARTER), 1) // HD
    spread = jnp.where(head == col, jnp.concatenate([query] * 4, 0), 0.0).astype(BF16)
    keyed = turn(expand(spread, QUARTER), back).astype(BF16)
    logits = []
    for copy, x in zip(copies[4:], xs):
        copy.wait()
        logits.append(mm_nt(keyed, x[: 2 * S]))
    logits = jnp.concatenate(logits, 1) * HD ** (-0.5)
    live = jnp.concatenate([x[2 * S : 2 * S + 1, : 2 * S].astype(F32) for x in xs], 1)
    pair, slot = iota((32, 8 * S), 0) % 8, iota((32, 8 * S), 1) // S
    logits = jnp.where((pair == slot) & (live > 0.5), logits, -1e30)
    weights = jnp.exp(logits - jnp.max(logits, -1, keepdims=True))
    weights = (weights / jnp.sum(weights, -1, keepdims=True)).astype(BF16)
    mixed = mm(weights[:, : 2 * S], xs[0][: 2 * S])
    for i in range(1, 4):
        mixed += mm(weights[:, i * 2 * S : (i + 1) * 2 * S], xs[i][: 2 * S])
    context = reduce(turn(mixed, there).astype(BF16), 2 * QUARTER)
    context = jnp.where(head == col, context, 0.0)
    context = (context[:8] + context[8:16] + context[16:24] + context[24:]).astype(BF16)
    projected = turn(expand(context, 3 * QUARTER), back)
    own = projected[:2] + lead[:2]
    core, far, both = projected[2:4], projected[4:6], projected[6:]
    for ref, order in (
        (near_ref, (own, core, far, both)),
        (flip_ref, (core, own, both, far)),
        (far_ref, (far, both, own, core)),
        (farflip_ref, (both, far, core, own)),
    ):
        ref[:, :DT] = jnp.concatenate(order, 0)
        ref[:, DT:] = student_ref[...]


def teacher_partial(y, xs, ws, student_scores):
    shape = jax.ShapeDtypeStruct((8, DT + 128), F32)
    vmem = pl.BlockSpec(memory_space=pltpu.VMEM)
    return pl.pallas_call(
        teacher_kernel,
        out_shape=(shape,) * 4,
        in_specs=[pl.BlockSpec(memory_space=pltpu.SMEM)]
        + [pl.BlockSpec(memory_space=pl.ANY)] * 8
        + [vmem],
        out_specs=(vmem,) * 4,
        scratch_shapes=[
            pltpu.VMEM((4, 2 * S + 16, DT), BF16),
            pltpu.VMEM((4, 2, 128, DT), BF16),
            pltpu.VMEM((4, 2, 16, DT), BF16),
            pltpu.SemaphoreType.DMA((4,)),
            pltpu.SemaphoreType.DMA((4,)),
            pltpu.SemaphoreType.DMA((4, 2)),
        ],
        compiler_params=params(24),
        cost_estimate=pl.CostEstimate(flops=10**9, bytes_accessed=6 * 10**6, transcendentals=0),
        name="teacher_partial",
    )(y.reshape(1), *xs, *ws, student_scores)


def score_kernel(own, core, far, both, gain, weight, tile_ref, spread_ref, score_ref):
    refs = (own, core, far, both)
    values = own[:, :DT] + core[:, :DT] + far[:, :DT] + both[:, :DT]
    centred = values - jnp.mean(values, -1, keepdims=True)
    unit = centred * lax.rsqrt(jnp.mean(centred * centred, -1, keepdims=True) + EPS)
    score = jnp.sum(unit * gain[...] * weight[...], -1, keepdims=True)
    student = jnp.concatenate([ref[:2, DT:] for ref in refs], 0)
    tile = jnp.where(iota((8, 128), 1) < 64, score, student)
    tile_ref[...] = tile
    for i in range(2):
        score_ref[i] = jnp.sum(score[i : i + 1])
    for i in range(16):
        spread_ref[i] = tile


def score_tile(parts, gain, weight):
    vmem = pl.BlockSpec(memory_space=pltpu.VMEM)
    return pl.pallas_call(
        score_kernel,
        out_shape=(
            jax.ShapeDtypeStruct((8, 128), F32),
            jax.ShapeDtypeStruct((16, 8, 128), F32),
            jax.ShapeDtypeStruct((2,), F32),
        ),
        in_specs=[vmem] * 6,
        out_specs=(vmem, vmem, pl.BlockSpec(memory_space=pltpu.SMEM)),
        compiler_params=params(8),
        name="score_tile",
    )(*parts, gain, weight)


def payload_kernel(
    half_ref, first_ref, tile_ref, all_ref, q_ref, p_ref, gp_hbm, first_hbm, recv_hbm, sums_ref, g_ref, out_hbm,
    gp, term, recv, out, gp_sems, term_sems, recv_sems, out_sems,
):
    def load_grad(k):
        cols = pl.ds(k * DS, DS)
        return pltpu.make_async_copy(gp_hbm.at[1, :, cols], gp.at[:, cols], gp_sems.at[k])

    def load_first(k):
        cols = pl.ds(k * DS, DS)
        return pltpu.make_async_copy(first_hbm.at[:, cols], term.at[:, cols], term_sems.at[k])

    def load_term(k):
        cols = pl.ds(k * DS, DS)
        return pltpu.make_async_copy(recv_hbm.at[:, :, cols], recv.at[:, :, cols], recv_sems.at[k])

    def save(k):
        cols = pl.ds(k * DS, DS) if k < 3 else pl.ds(WIDE, PAY - WIDE)
        return pltpu.make_async_copy(out.at[:, cols], out_hbm.at[:, cols], out_sems.at[k])

    load_grad(3).start()
    for k in range(3):
        load_grad(k).start()
        load_first(k).start()
        load_term(k).start()
    every = jnp.concatenate([all_ref[:, :4], all_ref[:, 4:]], 0)
    top = jnp.max(every, 0)
    lse = top + jnp.log(jnp.sum(jnp.exp(every - top[None]), 0))
    share = jnp.exp(tile_ref[:4] - lse)
    cot = LOSS_SCALE * (share[:, 64:65] - share[:, :1])
    rows = jnp.concatenate([q_ref[first_ref[0] + 1], p_ref[1]], 0)
    wide = select_features(half_ref[0], rows) * cot[1:2]
    main = wide.astype(BF16)
    by_group = jnp.concatenate([cot[j : j + 1] for j in range(2) for _ in range(2)], 0)
    scaled = sums_ref[...] * by_group[None]
    high = scaled.astype(BF16).astype(F32)
    scaled = jnp.where(iota((CHIPS, 4, 128), 2) < 64, high, scaled - high)
    scaled = jnp.concatenate([scaled, scaled], 1).reshape(8 * CHIPS, 128)
    out[:, WIDE : WIDE + 128] = scaled.astype(BF16)
    grad = g_ref[...].astype(F32)
    grad = jnp.concatenate([grad[:, : DS // 2], grad[:, DS // 2 :]], 0)
    out[:, WIDE + 128 :] = jnp.concatenate([grad] * CHIPS, 0).astype(BF16)
    save(3).start()
    load_grad(3).wait()
    for k in range(3):
        rest = late_features(wide, k)
        load_grad(k).wait()
        load_first(k).wait()
        load_term(k).wait()
        for part in range(3):
            cols = slice(k * DS + part * 256, k * DS + part * 256 + 256)
            late = slice(3 * DS + part * 256, 3 * DS + part * 256 + 256)
            total = mm(main, gp[:, cols]) + mm(rest, gp[:, late])
            total += term[:, cols].astype(F32) * cot[:1]
            for i in range(2):
                total += recv[i, :, cols].astype(F32) * cot[2 + i : 3 + i]
            out[:, cols] = total.astype(BF16)
        save(k).start()
    for k in range(4):
        save(k).wait()


def payload(half, first, tile, every, queries, passages, grad_pre, term, received, sums, grad):
    vmem = pl.BlockSpec(memory_space=pltpu.VMEM)
    anywhere = pl.BlockSpec(memory_space=pl.ANY)
    return pl.pallas_call(
        payload_kernel,
        out_shape=jax.ShapeDtypeStruct((CHIPS * 8, PAY), BF16),
        in_specs=[pl.BlockSpec(memory_space=pltpu.SMEM)] * 2
        + [vmem] * 4
        + [anywhere, anywhere, anywhere, vmem, vmem],
        out_specs=anywhere,
        scratch_shapes=[
            pltpu.VMEM((S, FF), BF16),
            pltpu.VMEM((8 * CHIPS, WIDE), BF16),
            pltpu.VMEM((2, 8 * CHIPS, WIDE), BF16),
            pltpu.VMEM((8 * CHIPS, PAY), BF16),
            pltpu.SemaphoreType.DMA((4,)),
            pltpu.SemaphoreType.DMA((3,)),
            pltpu.SemaphoreType.DMA((3,)),
            pltpu.SemaphoreType.DMA((4,)),
        ],
        compiler_params=params(60),
        name="payload",
    )(
        half.reshape(1), first.reshape(1), tile, every, queries, passages, grad_pre, term, received,
        sums, grad,
    )


def sum_kernel(in_ref, gin_ref):
    total = in_ref[0, :, :WIDE].astype(F32)
    for d in range(1, CHIPS):
        total += in_ref[d, :, :WIDE].astype(F32)
    gin_ref[:, :WIDE] = total[:6]
    for r in range(6):
        line, at = 6 + r // 3, r % 3 * DS
        gin_ref[r : r + 1, WIDE:] = total[line : line + 1, at : at + DS]


def sum_terms(incoming):
    vmem = pl.BlockSpec(memory_space=pltpu.VMEM)
    return pl.pallas_call(
        sum_kernel,
        out_shape=jax.ShapeDtypeStruct((6, FF), F32),
        in_specs=[vmem],
        out_specs=vmem,
        compiler_params=params(32),
        name="sum_terms",
    )(incoming)


def outer_kernel(core_ref, in_ref, own_ref, send_ref):
    columns = in_ref[:, :, WIDE : WIDE + 128].astype(F32).reshape(CHIPS * 8, 128).T
    line = iota((128, CHIPS * 8), 1) % 8
    grads = in_ref[:, :, WIDE + 128 :].astype(F32).reshape(CHIPS * 8, DS // 2).astype(BF16)
    left = mm(jnp.where(line < 4, columns, 0.0).astype(BF16), grads)
    right = mm(jnp.where(line < 4, 0.0, columns).astype(BF16), grads)
    both = jnp.concatenate([left[:48] + left[64:112], right[:48] + right[64:112]], 1)
    first = core_ref[0] == 0
    own_ref[...] = jnp.where(first, both[:24], both[24:])
    send_ref[...] = jnp.where(first, both[24:], both[:24])


def outer_terms(core, incoming):
    vmem = pl.BlockSpec(memory_space=pltpu.VMEM)
    part = jax.ShapeDtypeStruct((24, DS), F32)
    return pl.pallas_call(
        outer_kernel,
        out_shape=(part, part),
        in_specs=[pl.BlockSpec(memory_space=pltpu.SMEM), vmem],
        out_specs=(vmem,) * 2,
        compiler_params=params(32),
        name="outer_terms",
    )(core.reshape(1), incoming)


def pack_kernel(me_ref, qkv_ref, out_ref, p0, p1, p2, p3):
    for flip, ref in enumerate((p0, p1, p2, p3)):
        for j in range(4):

            @pl.when(me_ref[0] == j)
            def _():
                who = j ^ flip
                for t in range(3):
                    at = t * DT + who * QUARTER
                    ref[0, :, t * QUARTER : (t + 1) * QUARTER] = qkv_ref[:, at : at + QUARTER]
                ref[0, :, 3 * QUARTER :] = out_ref[:, who * QUARTER : (who + 1) * QUARTER]


def pack_weights(me, qkv_weight, out_weight):
    vmem = pl.BlockSpec(memory_space=pltpu.VMEM)
    return pl.pallas_call(
        pack_kernel,
        out_shape=(jax.ShapeDtypeStruct((1, 16, DT), BF16),) * 4,
        in_specs=[pl.BlockSpec(memory_space=pltpu.SMEM), vmem, vmem],
        out_specs=(vmem,) * 4,
        compiler_params=params(8),
        name="pack_weights",
    )(me.reshape(1), qkv_weight, out_weight.T)


def exchange_weights(qkv_weight, out_weight):
    me = 2 * lax.axis_index("zl") + lax.axis_index("c")
    mine, to_core, to_far, to_both = pack_weights(me, qkv_weight, out_weight)
    from_core = lax.ppermute(to_core, "c", SWAP)
    from_far = lax.ppermute(to_far, "zl", SWAP)
    from_both = lax.ppermute(to_both, ("zl", "c"), BOTH)
    four = jnp.zeros((4, 16, DT), BF16)
    for part, who in ((mine, me), (from_core, me ^ 1), (from_far, me ^ 2), (from_both, me ^ 3)):
        four = lax.dynamic_update_slice(four, part, (who, 0, 0))
    return four.reshape(2, 1, 1, 32, DT)


def body(
    teacher_hidden,
    passage_len,
    qkv_weight,
    out_weight,
    teacher_gain,
    score_weight,
    query_tokens,
    passage_tokens,
    w_in,
    w_out,
):
    core = lax.axis_index("c")
    first = lax.axis_index("xl") * 4 + core * 2

    slots = jnp.arange(S)
    live = (slots[None, :] < SQ) | (slots[None, :] - SQ < passage_len[:, None])
    live = jnp.pad(live.astype(BF16).reshape(1, 2 * S), ((0, 15), (0, DT - 2 * S)))
    hidden = jnp.concatenate([teacher_hidden.reshape(2 * S, DT), live], 0)

    four = exchange_weights(qkv_weight, out_weight)
    four, hidden = lax.optimization_barrier((four, hidden))
    hidden_far = lax.ppermute(hidden, "zl", SWAP)
    hidden_core = lax.ppermute(hidden, "c", SWAP)
    plane = join_axis(send_axis(four, X), X, 2)
    plane, early_query, hidden_core = lax.optimization_barrier((plane, query_tokens, hidden_core))
    planes = send_axis(plane, "y")

    sums, student_scores, grad, grad_pre, other = student(
        passage_len, 1 - core, first, early_query, passage_tokens, w_in, w_out
    )

    planes, other, hidden_far = lax.optimization_barrier((planes, other, hidden_far))
    hidden_both = lax.ppermute(hidden_far, "c", SWAP)
    here, before, after, across = [part.reshape(2, 128, DT) for part in planes]
    near, flip, far, farflip = teacher_partial(
        lax.axis_index("y"),
        (hidden, hidden_core, hidden_far, hidden_both),
        (here, after, across, before),
        student_scores,
    )
    parts = (
        near,
        lax.ppermute(flip, "c", SWAP),
        lax.ppermute(far, "zl", SWAP),
        lax.ppermute(farflip, ("zl", "c"), BOTH),
    )
    tile, spread, scores = score_tile(parts, teacher_gain[None], score_weight[None])
    every = lax.all_to_all(spread, RIVALS, 0, 0, tiled=True)
    other, late_query, _ = lax.optimization_barrier((other, query_tokens, tile))
    received = lax.ppermute(other, "c", SWAP)
    term = first_term(core, first, late_query, passage_tokens, grad_pre)
    outgoing = payload(
        core, first, tile, every, query_tokens, passage_tokens, grad_pre, term, received, sums, grad
    )
    incoming = lax.all_to_all(outgoing.reshape(CHIPS, 8, PAY), CHIP_AXES, 0, 0, tiled=True)
    own_out, send_out = outer_terms(core, incoming)
    grad_in = sum_terms(incoming)
    return (scores, grad_in, own_out + lax.ppermute(send_out, "c", SWAP))


def solution(mesh):
    fine = Mesh(mesh.devices.reshape(2, 2, 4, 2, 2, 2), AXES)
    placed = (
        P(AXES, None, None),
        P(AXES),
        P(DP, None),
        P(None, DP),
        P(),
        P(),
        P(),
        P(AXES, None, None),
        P(),
        P(),
    )
    return jax.shard_map(
        body,
        mesh=fine,
        in_specs=placed,
        out_specs=(P(AXES), P(AXES, None), P(AXES, None)),
        check_vma=False,
    )
```
